128 devices in a mesh: blk: 4 (over z_lo, core), grp: 32 (over x, y, z_hi).
Axes of the slice: x: 4, y: 4, z: 4 (z_hi: 2, z_lo: 2; z = z_hi * 2 + z_lo), core: 2. Of those that a mesh axis runs over, the one named last changes fastest.
Arguments:
- features: bfloat16 [131072, 1024], P(('blk', 'grp')), may hold values from -24 to 24
- tiles: bfloat16 [1024, 24, 128, 128], P(('blk', 'grp')), may hold values from 0 to 1, as said below
- slots: int32 [1024, 24], P(('blk', 'grp')), may hold values from 0 to 1023, as said below
- w_self: bfloat16 [1024, 1024], replicated, may hold values from -0.1875 to 0.1875
- w_neigh: bfloat16 [1024, 1024], replicated, may hold values from -0.375 to 0.375
- cotangent: bfloat16 [131072, 1024], P(('blk', 'grp')), may hold values from -0.016479492 to 0.016479492
Outputs:
- hidden: bfloat16 [131072, 1024], P(('blk', 'grp'))
- grad_self: float32 [1024, 1024], P(('blk', 'grp'))
- grad_neigh: float32 [1024, 1024], P(('blk', 'grp'))
The draws below stay inside these ranges and needn't reach their ends.
Inputs may be any that keep to these rules, and one draw needn't show every extreme that they name: Nodes are laid out device by device: device d = b * 32 + g (b the index of blk, g of grp) holds row blocks d * 8 onward. Each row block has a live count c of 1 to 24; slots 0 to c-1 name distinct column blocks, each held by the row block's own device or by device (b, g-1), (b, g+1), (b-1, g) or (b+1, g), indices taken modulo 32 and 4; slots c and after repeat slot 0. The first row block of every device has c = 24, and its live slots name column blocks of all five of those devices. Tiles of slots at or after a row block's live count are zero; live tiles have every entry positive, at least 0.05.
All inputs are finite; a program needn't handle non-finite values.
Results may differ from the reference program's by a relative error of at most 0.0049.
Values may be sent and summed in bfloat16 or wider, within the bound.
A program may use at most 128 MiB of HBM per device.

```python
import jax
import jax.numpy as jnp
from jax import lax

D_IN = 1024
D_OUT = 1024
BLOCK = 128
K_SLOTS = 24
ROWS = 1024
NODES = 131072
N_BLK = 4
N_GRP = 32


def shared_layout(key):
    row_blocks = NODES // BLOCK
    dev_blocks = ROWS // BLOCK
    first, second, third, fourth = jax.random.split(key, 4)
    live_a = jax.random.randint(first, (row_blocks,), 1, K_SLOTS + 1)
    live_b = jax.random.randint(second, (row_blocks,), 1, K_SLOTS + 1)
    live = jnp.minimum(live_a, live_b)
    row_index = jnp.arange(row_blocks, dtype=jnp.int32)
    leading = row_index % dev_blocks == 0
    live = jnp.where(leading, K_SLOTS, live)
    width = 5 * dev_blocks
    scores = jax.random.randint(third, (row_blocks, width), 0, 1 << 20)
    scores = scores * width + jnp.arange(width, dtype=jnp.int32)[None, :]
    forced_inner = jax.random.randint(fourth, (row_blocks, 5), 0, dev_blocks)
    forced = jnp.arange(5, dtype=jnp.int32)[None, :] * dev_blocks + forced_inner
    candidate = jnp.arange(width, dtype=jnp.int32)[None, None, :]
    marked = jnp.any(forced[:, :, None] == candidate, axis=1)
    marked = marked & leading[:, None]
    scores = jnp.where(marked, scores - (1 << 28), scores)
    order = jnp.argsort(scores, axis=1)[:, :K_SLOTS].astype(jnp.int32)
    which = order // dev_blocks
    inner = order % dev_blocks
    device = row_index // dev_blocks
    group = (device // N_GRP)[:, None]
    member = (device % N_GRP)[:, None]
    member_step = jnp.where(which == 1, N_GRP - 1, jnp.where(which == 2, 1, 0))
    group_step = jnp.where(which == 3, N_BLK - 1, jnp.where(which == 4, 1, 0))
    target = (group + group_step) % N_BLK * N_GRP + (member + member_step) % N_GRP
    chosen = target * dev_blocks + inner
    slot_pos = jnp.arange(K_SLOTS, dtype=jnp.int32)[None, :]
    chosen = jnp.where(slot_pos < live[:, None], chosen, chosen[:, :1])
    return (live, chosen.astype(jnp.int32))


def draw_slots(key, part):
    live, chosen = shared_layout(key)
    return chosen


def draw_tiles(key, part):
    live, chosen = shared_layout(key)
    key = jax.random.fold_in(key, 11)
    row_blocks = NODES // BLOCK
    first = jax.random.fold_in(key, 0)
    shape = (row_blocks, K_SLOTS, BLOCK, BLOCK)
    values = jnp.exp(jax.random.uniform(first, shape, jnp.float32, jnp.log(0.05), 0.0))
    slot_pos = jnp.arange(K_SLOTS, dtype=jnp.int32)[None, :]
    keep = (slot_pos < live[:, None]).astype(jnp.float32)
    return (values * keep[:, :, None, None]).astype(jnp.bfloat16)


def raised(drawn, own_key, source, target, shards_of, factor):
    def block_of(axis_at):
        return (jnp.arange(drawn.shape[axis_at]) // (drawn.shape[axis_at] // shards_of)).reshape((-1,) + (1,) * (drawn.ndim - 1 - axis_at))

    near = jax.random.permutation(own_key, shards_of)[block_of(target)]
    far = (block_of(target) + shards_of // 2) % shards_of
    return jnp.where((block_of(source) == near) | (block_of(source) == far), factor * drawn, drawn)


def block_scale(own_key, dims, cuts, least, largest):
    factor_of = 1.0
    for axis_at, shards_of in cuts:
        draws = jax.random.uniform(jax.random.fold_in(jax.random.fold_in(own_key, 6), axis_at), (shards_of,), jnp.float32, least / len(cuts), largest / len(cuts))
        factor_of = factor_of * jnp.repeat(jnp.exp(draws), dims[axis_at] // shards_of).reshape((-1,) + (1,) * (len(dims) - 1 - axis_at))
    return factor_of


def normal_values(own_key, shape, scale, reach, cuts=(), kind=jnp.bfloat16):
    array = scale * jax.random.normal(own_key, shape, jnp.float32)
    if cuts:
        array = array * block_scale(own_key, shape, cuts, -0.22, 0.18)
    return jnp.clip(array, -reach, reach).astype(kind)


def gaussian_with(own_key, extent, deviation, most, shards, heavy, kind=jnp.bfloat16):
    array = deviation * jax.random.normal(own_key, extent, jnp.float32)
    if shards:
        array = array * block_scale(own_key, extent, shards, -0.22, 0.18)
    return jnp.clip(raised(array, jax.random.fold_in(own_key, 3), *heavy), -most, most).astype(kind)


def setup_inputs(seed: int = 0) -> dict:
    keys = jax.random.split(jax.random.key(seed), 7)
    features = gaussian_with(keys[0], (NODES, D_IN), 1.0, 24.0, ((0, 128),), (0, 1, 128, 5.5))
    tiles = draw_tiles(jax.random.fold_in(keys[6], 71), 0)
    slots = draw_slots(jax.random.fold_in(keys[6], 71), 0)
    w_self = normal_values(keys[3], (D_IN, D_OUT), D_IN ** -0.5, 0.1875)
    w_neigh = normal_values(keys[4], (D_IN, D_OUT), (D_IN // 4) ** -0.5, 0.375)
    cotangent = normal_values(keys[5], (NODES, D_OUT), (NODES ** -0.5), 0.016479492, ((0, 128),))
    return {"features": features, "tiles": tiles, "slots": slots, "w_self": w_self, "w_neigh": w_neigh, "cotangent": cotangent}


def gelu_tanh(v):
    return jax.nn.gelu(v, approximate=True)

def reference(features, tiles, slots, w_self, w_neigh, cotangent):
    row_blocks = NODES // BLOCK
    blocked = features.reshape(row_blocks, BLOCK, D_IN)

    def one_block(pair):
        tile_set, slot_set = pair
        picked = blocked[slot_set].astype(jnp.float32)
        tile_f = tile_set.astype(jnp.float32)
        total = jnp.einsum('kab,kbf->af', tile_f, picked)
        degree = lax.optimization_barrier(jnp.sum(tile_f, axis=(0, 2)))
        return (total / degree[:, None]).astype(jnp.bfloat16)
    mean_neigh = lax.map(one_block, (tiles, slots)).reshape(NODES, D_IN)
    pre = jnp.dot(features, w_self, preferred_element_type=jnp.float32)
    pre = pre + jnp.dot(mean_neigh, w_neigh, preferred_element_type=jnp.float32)
    hidden = gelu_tanh(pre).astype(jnp.bfloat16)
    slope = jax.vjp(gelu_tanh, pre)[1]
    dpre = slope(cotangent.astype(jnp.float32))[0].astype(jnp.bfloat16)
    grad_self = jnp.dot(features.T, dpre, preferred_element_type=jnp.float32)
    grad_neigh = jnp.dot(mean_neigh.T, dpre, preferred_element_type=jnp.float32)
    return (hidden, grad_self, grad_neigh)
```

```python
import functools

import jax
import jax.numpy as jnp
from jax import lax
from jax.experimental import pallas as pl
from jax.experimental.pallas import tpu as pltpu
from jax.sharding import PartitionSpec as P

MESH = pl.DeviceIdType.MESH
BLOCK = 128
SLOTS = 24
ROWS = 1024
DIM = 1024
COLS = 256
CHUNKS = DIM // COLS
BLOCKS = ROWS // BLOCK
N_GRP = 32
PIECES = CHUNKS * BLOCKS
AHEAD = 4
UNITS = 2 * CHUNKS
F32 = jnp.float32
BF16 = jnp.bfloat16


def loop(count, body):
    lax.fori_loop(0, count, lambda i, _: (body(i), None)[1], None)


def kernel(
    inv_ref, feat_ref, tiles_ref, ws_ref, wn_ref, cot_ref,
    hidden_ref, gs_ref, gn_ref,
    src, adj, tbuf_even, tbuf_odd, ws, wn, cot, pre, total, feat_t, mean_t, mean, rinv, dpre, hid,
    core_out, core_in, s1_out, s1_in, acc1, s2_out, s2_in, acc2, s3_in,
    local_sem, tile_sem, hid_sem, fc_sem, fc_recv, f_send, f1_recv, f2_recv, f3_recv,
    core_send, core_recv, s1_send, s1_recv, s2_send, s2_recv, s3_send, s3_recv,
):
    b = lax.axis_index("blk")
    g = lax.axis_index("grp")
    z_lo = b // 2
    core = b % 2
    z_hi = g % 2
    y = (g // 2) % 4
    x = g // 8

    def at(bb, gg):
        return (bb, gg)

    core_peer = at(z_lo * 2 + (1 - core), g)
    z_peer = at(3 - b, g)
    hi_peer = at(3 - b, z_hi * (g - 1) + (1 - z_hi) * (g + 1))
    step = 2 - 4 * z_hi
    out_peer = at(b, (g + step + N_GRP) % N_GRP)
    in_peer = at(b, (g - step + N_GRP) % N_GRP)

    def x_peer(d):
        return at(b, ((x + d) % 4) * 8 + y * 2 + z_hi)

    def y_peer(d):
        return at(b, x * 8 + ((y + d) % 4) * 2 + z_hi)

    def z_ring(d):
        lo = (z_lo + d % 2) % 2
        hi = (z_hi + d // 2) % 2
        return lo, hi

    def z_dev(d):
        lo, hi = z_ring(d)
        return at(lo * 2 + core, x * 8 + y * 2 + hi)

    peers = [core_peer, z_peer, hi_peer, out_peer, in_peer]
    for d in (1, 2, 3):
        peers += [x_peer(d), y_peer(d), z_dev(d)]

    def feat_copy(c):
        return pltpu.make_async_copy(
            feat_ref.at[:, pl.ds(c * COLS, COLS)], src.at[0, c], local_sem.at[c])

    tile_bufs = (tbuf_even, tbuf_odd)

    def tile_copy(r, slot):
        return pltpu.make_async_copy(
            tiles_ref.at[r], tile_bufs[slot].at[pl.ds(0, SLOTS)], tile_sem.at[slot])

    ws_copy = pltpu.make_async_copy(ws_ref, ws, local_sem.at[4])
    wn_copy = pltpu.make_async_copy(wn_ref, wn, local_sem.at[5])
    cot_copy = pltpu.make_async_copy(cot_ref, cot, local_sem.at[6])

    barrier = pltpu.get_barrier_semaphore()
    for p in peers:
        pl.semaphore_signal(barrier, inc=1, device_id=p, device_id_type=MESH)
    tile_copy(0, 0).start()
    for c in range(CHUNKS):
        feat_copy(c).start()
    ws_copy.start()
    pl.semaphore_wait(barrier, len(peers))

    def piece(p):
        return p // BLOCKS, pl.ds(pl.multiple_of((p % BLOCKS) * BLOCK, BLOCK), BLOCK)

    def f1(p):
        c, rows = piece(p)
        return pltpu.make_async_remote_copy(
            src_ref=feat_ref.at[rows, pl.ds(pl.multiple_of(c * COLS, COLS), COLS)],
            dst_ref=src.at[2, c, rows],
            send_sem=f_send.at[0], recv_sem=f1_recv.at[p],
            device_id=z_peer, device_id_type=MESH)

    def f2(p):
        c, rows = piece(p)
        return pltpu.make_async_remote_copy(
            src_ref=src.at[2, c, rows], dst_ref=src.at[3, c, rows],
            send_sem=f_send.at[1], recv_sem=f2_recv.at[p],
            device_id=hi_peer, device_id_type=MESH)

    def f3(p):
        c, rows = piece(p)
        return pltpu.make_async_remote_copy(
            src_ref=src.at[3, c, rows], dst_ref=src.at[4, c, rows],
            send_sem=f_send.at[2], recv_sem=f3_recv.at[p],
            device_id=out_peer, device_id_type=MESH)

    def fc(c):
        return pltpu.make_async_remote_copy(
            src_ref=feat_ref.at[:, pl.ds(pl.multiple_of(c * COLS, COLS), COLS)],
            dst_ref=src.at[1, c],
            send_sem=fc_sem.at[c], recv_sem=fc_recv.at[c],
            device_id=core_peer, device_id_type=MESH)

    for p in range(AHEAD):
        f1(p).start()
    for c in range(CHUNKS):
        fc(c).start()
    wn_copy.start()
    cot_copy.start()
    zero_tile = jnp.zeros((BLOCK, BLOCK), BF16)
    tbuf_even[SLOTS] = zero_tile
    tbuf_odd[SLOTS] = zero_tile

    def build(r, slot):
        tbuf = tile_bufs[slot]

        @pl.when(r + 1 < BLOCKS)
        def _():
            tile_copy(r + 1, 1 - slot).start()

        tile_copy(r, slot).wait()
        rows = pl.ds(pl.multiple_of(r * BLOCK, BLOCK), BLOCK)

        def add(k, acc):
            return acc + tbuf[k].astype(F32)

        deg = lax.fori_loop(0, SLOTS, add, jnp.zeros((BLOCK, BLOCK), F32))
        deg = jnp.sum(deg, axis=1, keepdims=True)
        rinv[rows, :] = jnp.broadcast_to(1.0 / deg, (BLOCK, BLOCK))

        def place(s):
            for j in range(BLOCKS):
                k = inv_ref[r, s * BLOCKS + j]
                adj[s, rows, j * BLOCK:(j + 1) * BLOCK] = tbuf[k]

        loop(5, place)

    def product(s, c, first):
        def body(m):
            rows = pl.ds(pl.multiple_of(m * 256, 256), 256)
            part = jnp.dot(adj[s, rows, :], src[s, c], preferred_element_type=F32)
            if first:
                total[c, rows, :] = part
            else:
                total[c, rows, :] += part
        loop(4, body)

    def transpose_into(dst, c, rows, value):
        dst[pl.ds(pl.multiple_of(c * COLS, COLS), COLS), rows] = value.T

    def pre_self(c):
        feat_copy(c).wait()

        def body(i):
            q = i // 2
            rows = pl.ds(pl.multiple_of((i % 2) * 512, 512), 512)
            part = jnp.dot(
                src[0, c, rows, :],
                ws[pl.ds(pl.multiple_of(c * COLS, COLS), COLS),
                   pl.ds(pl.multiple_of(q * COLS, COLS), COLS)],
                preferred_element_type=F32)

            @pl.when(c == 0)
            def _():
                pre[q, rows, :] = part

            @pl.when(c > 0)
            def _():
                pre[q, rows, :] += part
        loop(8, body)

    def flip_features(c):
        def body(m):
            rows = pl.ds(pl.multiple_of(m * 256, 256), 256)
            transpose_into(feat_t, c, rows, src[0, c, rows, :])
        loop(4, body)

    def average(c):
        def scale(m):
            rows = pl.ds(pl.multiple_of(m * BLOCK, BLOCK), BLOCK)
            r = rinv[rows, :]
            value = (total[c, rows, :] * jnp.concatenate([r, r], axis=1)).astype(BF16)
            mean[rows, :] = value
            transpose_into(mean_t, c, rows, value)
        loop(BLOCKS, scale)

        def body(i):
            q = i // 2
            rows = pl.ds(pl.multiple_of((i % 2) * 512, 512), 512)
            pre[q, rows, :] += jnp.dot(
                mean[rows, :],
                wn[pl.ds(pl.multiple_of(c * COLS, COLS), COLS),
                   pl.ds(pl.multiple_of(q * COLS, COLS), COLS)],
                preferred_element_type=F32)
        loop(8, body)

    def tick(t):
        @pl.when(t < PIECES)
        def _():
            f1(t).wait_recv()
            f2(t).start()

        @pl.when(t + AHEAD < PIECES)
        def _():
            f1(t + AHEAD).start()

        @pl.when((t >= 2) & (t < PIECES + 2))
        def _():
            f2(t - 2).wait_recv()
            f3(t - 2).start()

        @pl.when((t >= 4) & (t < PIECES + 4))
        def _():
            f3(t - 4).wait_recv()

        phase = t // 8
        i = t % 8

        @pl.when(t == 0)
        def _():
            ws_copy.wait()

        @pl.when(t < 4)
        def _():
            build(2 * t, 0)
            build(2 * t + 1, 1)
            pre_self(t)

        @pl.when((t >= 4) & (t < 8))
        def _():
            flip_features(t - 4)

        @pl.when(i == 6)
        def _():
            product(0, phase, True)

        @pl.when(i == 7)
        def _():
            fc(phase).wait_recv()
            product(1, phase, False)

        @pl.when((t >= 8) & (i < 5) & (i % 2 == 0))
        def _():
            product(2 + i // 2, phase - 1, False)

        @pl.when(t == 8)
        def _():
            wn_copy.wait()

        @pl.when((t >= 8) & (i == 5))
        def _():
            average(phase - 1)

    loop(PIECES + 6, tick)

    cot_copy.wait()
    c0 = 0.7978845608028654
    c1 = 0.044715

    def hid_copy(q):
        return pltpu.make_async_copy(
            hid.at[q], hidden_ref.at[:, pl.ds(pl.multiple_of(q * COLS, COLS), COLS)],
            hid_sem.at[q])

    def gelu(q):
        cols = pl.ds(pl.multiple_of(q * COLS, COLS), COLS)

        def body(m):
            rows = pl.ds(pl.multiple_of(m * 64, 64), 64)
            v = pre[q, rows, :]
            v2 = v * v
            th = jnp.tanh(c0 * (v + c1 * (v2 * v)))
            half = 0.5 * (1.0 + th)
            hid[q, rows, :] = (v * half).astype(BF16)
            slope = half + (0.5 * v) * (1.0 - th * th) * (c0 + (3.0 * c0 * c1) * v2)
            dpre[rows, :] = (cot[rows, cols].astype(F32) * slope).astype(BF16)
        loop(16, body)
        hid_copy(q).start()

    def keep_rows(u, first, count):
        return (u // 2, pl.ds(pl.multiple_of((u % 2) * 512 + first, 8), count))

    def core_copy(u):
        return pltpu.make_async_remote_copy(
            src_ref=core_out.at[u], dst_ref=core_in.at[u],
            send_sem=core_send.at[u], recv_sem=core_recv.at[u],
            device_id=core_peer, device_id_type=MESH)

    def gradient(q, kind):
        u = 2 * q + kind
        left = feat_t if kind == 0 else mean_t

        def body(lo):
            other = pl.ds(pl.multiple_of(lo * 512 + (1 - core) * 256, 256), 256)
            core_out[u, lo] = jnp.dot(
                left[other, :], dpre[...], preferred_element_type=F32).astype(BF16)
        loop(2, body)
        core_copy(u).start()

        def body2(lo):
            mine = pl.ds(pl.multiple_of(lo * 512 + core * 256, 256), 256)
            qq, rows = keep_rows(u, lo * 256, 256)
            total[qq, rows, :] = jnp.dot(left[mine, :], dpre[...], preferred_element_type=F32)
        loop(2, body2)

    def s1(u, kind, d):
        return pltpu.make_async_remote_copy(
            src_ref=s1_out.at[u, d - 1], dst_ref=s1_in.at[u, d - 1],
            send_sem=s1_send.at[u, d - 1], recv_sem=s1_recv.at[u, d - 1],
            device_id=(x_peer if kind == 0 else y_peer)(d), device_id_type=MESH)

    def s2(u, kind, d):
        return pltpu.make_async_remote_copy(
            src_ref=s2_out.at[u, d - 1], dst_ref=s2_in.at[u, d - 1],
            send_sem=s2_send.at[u, d - 1], recv_sem=s2_recv.at[u, d - 1],
            device_id=(y_peer if kind == 0 else x_peer)(d), device_id_type=MESH)

    def s3(u, d):
        lo, hi = z_ring(d)
        return pltpu.make_async_remote_copy(
            src_ref=acc2.at[u, lo, pl.ds(pl.multiple_of(hi * 8, 8), 8)],
            dst_ref=s3_in.at[u, d - 1],
            send_sem=s3_send.at[u, d - 1], recv_sem=s3_recv.at[u, d - 1],
            device_id=z_dev(d), device_id_type=MESH)

    def half_rows(u, kind, lo, pos):
        if kind == 0:
            first = lo * 256 + pos * 64
            qq, rows = keep_rows(u, first, 64)
            inner = pl.ds(pl.multiple_of(pos * 64, 64), 64)
            return total[qq, rows, :] + core_in[u, lo, inner, :].astype(F32)
        parts = []
        for xx in range(4):
            first = lo * 256 + xx * 64 + pos * 16
            qq, rows = keep_rows(u, first, 16)
            inner = pl.ds(pl.multiple_of(xx * 64 + pos * 16, 16), 16)
            parts.append(total[qq, rows, :] + core_in[u, lo, inner, :].astype(F32))
        return jnp.concatenate(parts, axis=0)

    def stage1(q, kind):
        u = 2 * q + kind
        me = x if kind == 0 else y
        core_copy(u).wait_recv()
        for d in (1, 2, 3):
            for lo in range(2):
                s1_out[u, d - 1, lo] = half_rows(u, kind, lo, (me + d) % 4).astype(BF16)
            s1(u, kind, d).start()
        for lo in range(2):
            acc1[u, lo] = half_rows(u, kind, lo, me)

    def stage2(q, kind):
        u = 2 * q + kind
        me = y if kind == 0 else x
        for d in (1, 2, 3):
            s1(u, kind, d).wait_recv()
        for lo in range(2):
            acc = acc1[u, lo]
            for d in (1, 2, 3):
                acc = acc + s1_in[u, d - 1, lo].astype(F32)
            acc1[u, lo] = acc
        for d in (1, 2, 3):
            pos = (me + d) % 4
            for lo in range(2):
                s2_out[u, d - 1, lo] = acc1[
                    u, lo, pl.ds(pl.multiple_of(pos * 16, 16), 16), :].astype(BF16)
            s2(u, kind, d).start()

    def stage3(q, kind):
        u = 2 * q + kind
        me = y if kind == 0 else x
        for d in (1, 2, 3):
            s2(u, kind, d).wait_recv()
        for lo in range(2):
            acc = acc1[u, lo, pl.ds(pl.multiple_of(me * 16, 16), 16), :]
            for d in (1, 2, 3):
                acc = acc + s2_in[u, d - 1, lo].astype(F32)
            acc2[u, lo] = acc
        for d in (1, 2, 3):
            s3(u, d).start()

    def stage4(q, kind):
        u = 2 * q + kind
        out = gs_ref if kind == 0 else gn_ref
        for d in (1, 2, 3):
            s3(u, d).wait_recv()
        acc = acc2[u, z_lo, pl.ds(pl.multiple_of(z_hi * 8, 8), 8), :]
        for d in (1, 2, 3):
            acc = acc + s3_in[u, d - 1]
        out[:, pl.ds(pl.multiple_of(q * COLS, COLS), COLS)] = acc

    def tail(q):
        @pl.when(q < CHUNKS)
        def _():
            gelu(q)
            gradient(q, 0)

        @pl.when(q > 0)
        def _():
            stage1(q - 1, 1)

        @pl.when(q < CHUNKS)
        def _():
            gradient(q, 1)
            stage1(q, 0)

    loop(CHUNKS + 1, tail)

    def each(f):
        def body(q):
            f(q, 0)
            f(q, 1)
        loop(CHUNKS, body)

    each(stage2)
    each(stage3)
    each(stage4)

    for i in range(3):
        pltpu.make_async_copy(src.at[i + 2], src.at[i + 2], f_send.at[i]).wait()

    def done(q):
        fc(q).wait_send()
        hid_copy(q).wait()
        for kind in range(2):
            u = 2 * q + kind
            core_copy(u).wait_send()
            for d in (1, 2, 3):
                s1(u, kind, d).wait_send()
                s2(u, kind, d).wait_send()
                s3(u, d).wait_send()
    loop(CHUNKS, done)


def fused(inv, features, tiles, w_self, w_neigh, cotangent):
    any_space = pl.BlockSpec(memory_space=pl.ANY)
    vmem = pl.BlockSpec(memory_space=pltpu.VMEM)
    dma = pltpu.SemaphoreType.DMA
    scratch = [
        pltpu.VMEM((5, CHUNKS, ROWS, COLS), BF16),
        pltpu.VMEM((5, ROWS, ROWS), BF16),
        pltpu.VMEM((SLOTS + 1, BLOCK, BLOCK), BF16),
        pltpu.VMEM((SLOTS + 1, BLOCK, BLOCK), BF16),
        pltpu.VMEM((DIM, DIM), BF16),
        pltpu.VMEM((DIM, DIM), BF16),
        pltpu.VMEM((ROWS, DIM), BF16),
        pltpu.VMEM((CHUNKS, ROWS, COLS), F32),
        pltpu.VMEM((CHUNKS, ROWS, COLS), F32),
        pltpu.VMEM((DIM, ROWS), BF16),
        pltpu.VMEM((DIM, ROWS), BF16),
        pltpu.VMEM((ROWS, COLS), BF16),
        pltpu.VMEM((ROWS, BLOCK), F32),
        pltpu.VMEM((ROWS, COLS), BF16),
        pltpu.VMEM((CHUNKS, ROWS, COLS), BF16),
        pltpu.VMEM((UNITS, 2, 256, COLS), BF16),
        pltpu.VMEM((UNITS, 2, 256, COLS), BF16),
        pltpu.VMEM((UNITS, 3, 2, 64, COLS), BF16),
        pltpu.VMEM((UNITS, 3, 2, 64, COLS), BF16),
        pltpu.VMEM((UNITS, 2, 64, COLS), F32),
        pltpu.VMEM((UNITS, 3, 2, 16, COLS), BF16),
        pltpu.VMEM((UNITS, 3, 2, 16, COLS), BF16),
        pltpu.VMEM((UNITS, 2, 16, COLS), F32),
        pltpu.VMEM((UNITS, 3, 8, COLS), F32),
        dma((7,)), dma((2,)), dma((CHUNKS,)), dma((CHUNKS,)), dma((CHUNKS,)),
        dma((3,)), dma((PIECES,)), dma((PIECES,)), dma((PIECES,)),
        dma((UNITS,)), dma((UNITS,)),
        dma((UNITS, 3)), dma((UNITS, 3)), dma((UNITS, 3)), dma((UNITS, 3)),
        dma((UNITS, 3)), dma((UNITS, 3)),
    ]
    return pl.pallas_call(
        kernel,
        out_shape=(
            jax.ShapeDtypeStruct((ROWS, DIM), BF16),
            jax.ShapeDtypeStruct((8, DIM), F32),
            jax.ShapeDtypeStruct((8, DIM), F32),
        ),
        in_specs=[pl.BlockSpec(memory_space=pltpu.SMEM)] + [any_space] * 5,
        out_specs=(any_space, vmem, vmem),
        scratch_shapes=scratch,
        compiler_params=pltpu.CompilerParams(
            collective_id=0, has_side_effects=True, vmem_limit_bytes=62 * 1024 * 1024),
        cost_estimate=pl.CostEstimate(
            flops=20_000_000_000, bytes_accessed=20_000_000, transcendentals=1_000_000),
    )(inv, features, tiles, w_self, w_neigh, cotangent)


def slot_of(slots):
    b = lax.axis_index("blk")
    g = lax.axis_index("grp")
    flip = g + 1 - 2 * (g % 2)
    other = (g - 1 + 2 * (g % 2)) % N_GRP
    devices = jnp.stack([
        b * N_GRP + g, (b + 1 - 2 * (b % 2)) * N_GRP + g, (3 - b) * N_GRP + g,
        b * N_GRP + flip, b * N_GRP + other])
    wanted = (devices[:, None] * BLOCKS + jnp.arange(BLOCKS)[None, :]).reshape(-1)
    match = slots[:, None, :] == wanted[None, :, None]
    place = jnp.arange(SLOTS, dtype=jnp.int32)[None, None, :]
    return jnp.min(jnp.where(match, place, SLOTS), axis=2).astype(jnp.int32)


def on_device(features, tiles, slots, w_self, w_neigh, cotangent):
    return fused(slot_of(slots), features, tiles, w_self, w_neigh, cotangent)


def solution(mesh):
    in_specs = (
        P(("blk", "grp"), None),
        P(("blk", "grp"), None, None, None),
        P(("blk", "grp"), None),
        P(),
        P(),
        P(("blk", "grp"), None),
    )
    out_specs = (P(("blk", "grp"), None), P(("blk", "grp"), None), P(("blk", "grp"), None))
    return jax.shard_map(
        on_device, mesh=mesh, in_specs=in_specs, out_specs=out_specs, check_vma=False
    )
```

```python
import functools

import jax
import jax.numpy as jnp
from jax import lax
from jax.experimental import pallas as pl
from jax.experimental.pallas import tpu as pltpu
from jax.sharding import PartitionSpec as P

MESH = pl.DeviceIdType.MESH
BLOCK = 128
SLOTS = 24
ROWS = 1024
DIM = 1024
COLS = 256
CHUNKS = DIM // COLS
BLOCKS = ROWS // BLOCK
N_GRP = 32
PIECES = CHUNKS * BLOCKS
AHEAD = 8
LAG = 3
UNITS = 2 * CHUNKS
F32 = jnp.float32
BF16 = jnp.bfloat16


def loop(count, body):
    lax.fori_loop(0, count, lambda i, _: (body(i), None)[1], None)


def kernel(
    inv_ref, feat_ref, tiles_ref, ws_ref, wn_ref, cot_ref,
    hidden_ref, gs_ref, gn_ref,
    src, adj, tbuf_even, tbuf_odd, ws, wn, cot, pre, total, feat_t, mean_t, mean, rinv, dpre_even, dpre_odd, hid,
    core_out, core_in, s1_out, s1_in, acc1, s2_out, s2_in, acc2, s3_in,
    local_sem, tile_sem, hid_sem, fc_sem, fc_recv, f_send, f1_recv, f2_recv, f3_recv,
    core_send, core_recv, s1_send, s1_recv, s2_send, s2_recv, s3_send, s3_recv,
):
    b = lax.axis_index("blk")
    g = lax.axis_index("grp")
    z_lo = b // 2
    core = b % 2
    z_hi = g % 2
    y = (g // 2) % 4
    x = g // 8

    def at(bb, gg):
        return (bb, gg)

    core_peer = at(z_lo * 2 + (1 - core), g)
    z_peer = at(3 - b, g)
    hi_peer = at(3 - b, z_hi * (g - 1) + (1 - z_hi) * (g + 1))
    step = 2 - 4 * z_hi
    out_peer = at(b, (g + step + N_GRP) % N_GRP)
    in_peer = at(b, (g - step + N_GRP) % N_GRP)

    def x_peer(d):
        return at(b, ((x + d) % 4) * 8 + y * 2 + z_hi)

    def y_peer(d):
        return at(b, x * 8 + ((y + d) % 4) * 2 + z_hi)

    def z_ring(d):
        lo = (z_lo + d % 2) % 2
        hi = (z_hi + d // 2) % 2
        return lo, hi

    def z_dev(d):
        lo, hi = z_ring(d)
        return at(lo * 2 + core, x * 8 + y * 2 + hi)

    peers = [core_peer, z_peer, hi_peer, out_peer, in_peer]
    for d in (1, 2, 3):
        peers += [x_peer(d), y_peer(d), z_dev(d)]

    def feat_copy(c):
        return pltpu.make_async_copy(
            feat_ref.at[:, pl.ds(c * COLS, COLS)], src.at[0, c], local_sem.at[c])

    tile_bufs = (tbuf_even, tbuf_odd)

    def tile_copy(r, slot):
        return pltpu.make_async_copy(
            tiles_ref.at[r], tile_bufs[slot].at[pl.ds(0, SLOTS)], tile_sem.at[slot])

    ws_copy = pltpu.make_async_copy(ws_ref, ws, local_sem.at[4])
    wn_copy = pltpu.make_async_copy(wn_ref, wn, local_sem.at[5])
    cot_copy = pltpu.make_async_copy(cot_ref, cot, local_sem.at[6])

    barrier = pltpu.get_barrier_semaphore()
    for p in peers:
        pl.semaphore_signal(barrier, inc=1, device_id=p, device_id_type=MESH)
    tile_copy(0, 0).start()
    for c in range(CHUNKS):
        feat_copy(c).start()
    ws_copy.start()
    pl.semaphore_wait(barrier, len(peers))

    def piece(p):
        return p // BLOCKS, pl.ds(pl.multiple_of((p % BLOCKS) * BLOCK, BLOCK), BLOCK)

    def f1(p):
        c, rows = piece(p)
        return pltpu.make_async_remote_copy(
            src_ref=feat_ref.at[rows, pl.ds(pl.multiple_of(c * COLS, COLS), COLS)],
            dst_ref=src.at[2, c, rows],
            send_sem=f_send.at[0], recv_sem=f1_recv.at[p],
            device_id=z_peer, device_id_type=MESH)

    def f2(p):
        c, rows = piece(p)
        return pltpu.make_async_remote_copy(
            src_ref=src.at[2, c, rows], dst_ref=src.at[3, c, rows],
            send_sem=f_send.at[1], recv_sem=f2_recv.at[p],
            device_id=hi_peer, device_id_type=MESH)

    def f3(p):
        c, rows = piece(p)
        return pltpu.make_async_remote_copy(
            src_ref=src.at[3, c, rows], dst_ref=src.at[4, c, rows],
            send_sem=f_send.at[2], recv_sem=f3_recv.at[p],
            device_id=out_peer, device_id_type=MESH)

    def fc(c):
        return pltpu.make_async_remote_copy(
            src_ref=feat_ref.at[:, pl.ds(pl.multiple_of(c * COLS, COLS), COLS)],
            dst_ref=src.at[1, c],
            send_sem=fc_sem.at[c], recv_sem=fc_recv.at[c],
            device_id=core_peer, device_id_type=MESH)

    for p in range(AHEAD):
        f1(p).start()
    for c in range(CHUNKS):
        fc(c).start()
    wn_copy.start()
    cot_copy.start()
    zero_tile = jnp.zeros((BLOCK, BLOCK), BF16)
    tbuf_even[SLOTS] = zero_tile
    tbuf_odd[SLOTS] = zero_tile

    def build(r, slot):
        tbuf = tile_bufs[slot]

        @pl.when(r + 1 < BLOCKS)
        def _():
            tile_copy(r + 1, 1 - slot).start()

        tile_copy(r, slot).wait()
        rows = pl.ds(pl.multiple_of(r * BLOCK, BLOCK), BLOCK)

        def add(k, acc):
            for n in range(4):
                acc = acc + tbuf[4 * k + n].astype(F32)
            return acc

        deg = lax.fori_loop(0, SLOTS // 4, add, jnp.zeros((BLOCK, BLOCK), F32))
        deg = jnp.sum(deg, axis=1, keepdims=True)
        rinv[rows, :] = jnp.broadcast_to(1.0 / deg, (BLOCK, BLOCK))

        def place(s):
            for j in range(BLOCKS):
                k = inv_ref[r, s * BLOCKS + j]
                adj[s, rows, j * BLOCK:(j + 1) * BLOCK] = tbuf[k]

        loop(5, place)

    def product(s, c, first):
        part = jnp.dot(adj[s], src[s, c], preferred_element_type=F32)
        if first:
            total[c] = part
        else:
            total[c] += part

    def chunk(c):
        return pl.ds(pl.multiple_of(c * COLS, COLS), COLS)

    def pre_self(c):
        def body(q):
            part = jnp.dot(src[0, c], ws[chunk(c), chunk(q)], preferred_element_type=F32)

            @pl.when(c == 0)
            def _():
                pre[q] = part

            @pl.when(c > 0)
            def _():
                pre[q] += part
        loop(CHUNKS, body)

    def pre_neigh(c, q):
        pre[q] += jnp.dot(mean[...], wn[chunk(c), chunk(q)], preferred_element_type=F32)

    def flipped(c):
        turn = (c + core) % 2
        return pl.ds(pl.multiple_of(turn * 512 + (c // 2) * 256, 256), 256)

    def flip_features(c):
        feat_t[flipped(c), :] = src[0, c].T

    def average(c):
        def scale(m):
            rows = pl.ds(pl.multiple_of(m * 256, 256), 256)
            r = rinv[rows, :]
            value = (total[c, rows, :] * jnp.concatenate([r, r], axis=1)).astype(BF16)
            mean[rows, :] = value
        loop(4, scale)
        mean_t[flipped(c), :] = mean[...].T

    def tick(t):
        @pl.when(t < PIECES)
        def _():
            f1(t).wait_recv()
            f2(t).start()

        @pl.when(t + AHEAD < PIECES)
        def _():
            f1(t + AHEAD).start()

        @pl.when((t >= LAG) & (t < PIECES + LAG))
        def _():
            f2(t - LAG).wait_recv()
            f3(t - LAG).start()

        @pl.when(t >= 2 * LAG)
        def _():
            f3(t - 2 * LAG).wait_recv()

        phase = t // 8
        i = t % 8

        @pl.when((t < 8) & (i % 2 == 0))
        def _():
            build(t, 0)

        @pl.when((t < 8) & (i % 2 == 1))
        def _():
            build(t, 1)

        @pl.when((t < PIECES) & (((t >= 7) & (i == 1)) | (t == 8)))
        def _():
            product(0, phase - (t == 8).astype(jnp.int32), True)

        @pl.when((t < PIECES) & (((t >= 7) & (i == 4)) | (t == 8)))
        def _():
            c = phase - (t == 8).astype(jnp.int32)
            fc(c).wait_recv()
            product(1, c, False)

        @pl.when((t >= 8) & ((i == 0) | (i == 3) | (i == 5)))
        def _():
            product(2 + i // 2, phase - 1, False)

        @pl.when((t == 10) | (t == 15) | (t == 18) | (t == 23))
        def _():
            c = (t - 10) // 4

            @pl.when(c == 0)
            def _():
                ws_copy.wait()
                wn_copy.wait()

            pre_self(c)
            flip_features(c)

        @pl.when((t >= 8) & (t < PIECES) & (i == 6))
        def _():
            average(phase - 1)
            loop(CHUNKS, lambda q: pre_neigh(phase - 1, q))

    for c in range(CHUNKS):
        feat_copy(c).wait()
    loop(PIECES + 2 * LAG, tick)
    average(CHUNKS - 1)
    cot_copy.wait()

    c0 = 0.7978845608028654
    c1 = 0.044715

    dpre = (dpre_even, dpre_odd)

    def hid_copy(q):
        return pltpu.make_async_copy(
            hid.at[q], hidden_ref.at[:, pl.ds(pl.multiple_of(q * COLS, COLS), COLS)],
            hid_sem.at[q])

    def gelu(q):
        dp = dpre[q % 2]
        for m in range(16):
            rows = slice(m * 64, m * 64 + 64)
            v = pre[q, rows, :]
            v2 = v * v
            th = jnp.tanh(c0 * (v + c1 * (v2 * v)))
            half = 0.5 * (1.0 + th)
            hid[q, rows, :] = (v * half).astype(BF16)
            slope = half + (0.5 * v) * (1.0 - th * th) * (c0 + (3.0 * c0 * c1) * v2)
            given = cot[rows, q * COLS:(q + 1) * COLS].astype(F32)
            dp[rows, :] = (given * slope).astype(BF16)

    def keep_rows(u, first, count):
        return (u // 2, pl.ds(pl.multiple_of((u % 2) * 512 + first, 8), count))

    def core_copy(u):
        return pltpu.make_async_remote_copy(
            src_ref=core_out.at[u], dst_ref=core_in.at[u],
            send_sem=core_send.at[u], recv_sem=core_recv.at[u],
            device_id=core_peer, device_id_type=MESH)

    def gradient(q, kind):
        u = 2 * q + kind
        left = feat_t if kind == 0 else mean_t
        grad = jnp.dot(left[...], dpre[q % 2][...], preferred_element_type=F32)
        total[u // 2, (u % 2) * 512:(u % 2) * 512 + 512, :] = grad[:512]
        core_out[u] = grad[512:].reshape(2, 256, COLS).astype(BF16)

    def s1(u, kind, d):
        return pltpu.make_async_remote_copy(
            src_ref=s1_out.at[u, d - 1], dst_ref=s1_in.at[u, d - 1],
            send_sem=s1_send.at[u, d - 1], recv_sem=s1_recv.at[u, d - 1],
            device_id=(x_peer if kind == 0 else y_peer)(d), device_id_type=MESH)

    def s2(u, kind, d):
        return pltpu.make_async_remote_copy(
            src_ref=s2_out.at[u, d - 1], dst_ref=s2_in.at[u, d - 1],
            send_sem=s2_send.at[u, d - 1], recv_sem=s2_recv.at[u, d - 1],
            device_id=(y_peer if kind == 0 else x_peer)(d), device_id_type=MESH)

    def s3(u, d):
        lo, hi = z_ring(d)
        return pltpu.make_async_remote_copy(
            src_ref=acc2.at[u, lo, pl.ds(pl.multiple_of(hi * 8, 8), 8)],
            dst_ref=s3_in.at[u, d - 1],
            send_sem=s3_send.at[u, d - 1], recv_sem=s3_recv.at[u, d - 1],
            device_id=z_dev(d), device_id_type=MESH)

    def half_rows(u, kind, lo, pos):
        if kind == 0:
            first = lo * 256 + pos * 64
            qq, rows = keep_rows(u, first, 64)
            inner = pl.ds(pl.multiple_of(pos * 64, 64), 64)
            return total[qq, rows, :] + core_in[u, lo, inner, :].astype(F32)
        parts = []
        for xx in range(4):
            first = lo * 256 + xx * 64 + pos * 16
            qq, rows = keep_rows(u, first, 16)
            inner = pl.ds(pl.multiple_of(xx * 64 + pos * 16, 16), 16)
            parts.append(total[qq, rows, :] + core_in[u, lo, inner, :].astype(F32))
        return jnp.concatenate(parts, axis=0)

    def stage1(q, kind):
        u = 2 * q + kind
        me = x if kind == 0 else y
        core_copy(u).wait_recv()
        for d in (1, 2, 3):
            for lo in range(2):
                s1_out[u, d - 1, lo] = half_rows(u, kind, lo, (me + d) % 4).astype(BF16)
            s1(u, kind, d).start()
        for lo in range(2):
            acc1[u, lo] = half_rows(u, kind, lo, me)

    def stage2(q, kind):
        u = 2 * q + kind
        me = y if kind == 0 else x
        for d in (1, 2, 3):
            s1(u, kind, d).wait_recv()
        for lo in range(2):
            acc = acc1[u, lo]
            for d in (1, 2, 3):
                acc = acc + s1_in[u, d - 1, lo].astype(F32)
            acc1[u, lo] = acc
        for d in (1, 2, 3):
            pos = (me + d) % 4
            for lo in range(2):
                s2_out[u, d - 1, lo] = acc1[
                    u, lo, pl.ds(pl.multiple_of(pos * 16, 16), 16), :].astype(BF16)
            s2(u, kind, d).start()

    def stage3(q, kind):
        u = 2 * q + kind
        me = y if kind == 0 else x
        for d in (1, 2, 3):
            s2(u, kind, d).wait_recv()
        for lo in range(2):
            acc = acc1[u, lo, pl.ds(pl.multiple_of(me * 16, 16), 16), :]
            for d in (1, 2, 3):
                acc = acc + s2_in[u, d - 1, lo].astype(F32)
            acc2[u, lo] = acc
        for d in (1, 2, 3):
            s3(u, d).start()

    def stage4(q, kind):
        u = 2 * q + kind
        out = gs_ref if kind == 0 else gn_ref
        for d in (1, 2, 3):
            s3(u, d).wait_recv()
        acc = acc2[u, z_lo, pl.ds(pl.multiple_of(z_hi * 8, 8), 8), :]
        for d in (1, 2, 3):
            acc = acc + s3_in[u, d - 1]
        out[:, pl.ds(pl.multiple_of(q * COLS, COLS), COLS)] = acc

    pre_neigh(CHUNKS - 1, 0)
    gelu(0)
    for q in range(CHUNKS):
        if q + 1 < CHUNKS:
            pre_neigh(CHUNKS - 1, q + 1)
            gelu(q + 1)
        gradient(q, 0)
        gradient(q, 1)
        hid_copy(q).start()
        core_copy(2 * q).start()
        core_copy(2 * q + 1).start()
        if q > 0:
            stage1(q - 1, 0)
            stage1(q - 1, 1)
    stage1(CHUNKS - 1, 0)
    stage1(CHUNKS - 1, 1)

    def each(f):
        def body(q):
            f(q, 0)
            f(q, 1)
        loop(CHUNKS, body)

    each(stage2)
    each(stage3)
    each(stage4)

    for i in range(3):
        pltpu.make_async_copy(src.at[i + 2], src.at[i + 2], f_send.at[i]).wait()

    def done(q):
        fc(q).wait_send()
        hid_copy(q).wait()
        for kind in range(2):
            u = 2 * q + kind
            core_copy(u).wait_send()
            for d in (1, 2, 3):
                s1(u, kind, d).wait_send()
                s2(u, kind, d).wait_send()
                s3(u, d).wait_send()
    loop(CHUNKS, done)


def fused(inv, features, tiles, w_self, w_neigh, cotangent):
    any_space = pl.BlockSpec(memory_space=pl.ANY)
    vmem = pl.BlockSpec(memory_space=pltpu.VMEM)
    dma = pltpu.SemaphoreType.DMA
    scratch = [
        pltpu.VMEM((5, CHUNKS, ROWS, COLS), BF16),
        pltpu.VMEM((5, ROWS, ROWS), BF16),
        pltpu.VMEM((SLOTS + 1, BLOCK, BLOCK), BF16),
        pltpu.VMEM((SLOTS + 1, BLOCK, BLOCK), BF16),
        pltpu.VMEM((DIM, DIM), BF16),
        pltpu.VMEM((DIM, DIM), BF16),
        pltpu.VMEM((ROWS, DIM), BF16),
        pltpu.VMEM((CHUNKS, ROWS, COLS), F32),
        pltpu.VMEM((CHUNKS, ROWS, COLS), F32),
        pltpu.VMEM((DIM, ROWS), BF16),
        pltpu.VMEM((DIM, ROWS), BF16),
        pltpu.VMEM((ROWS, COLS), BF16),
        pltpu.VMEM((ROWS, BLOCK), F32),
        pltpu.VMEM((ROWS, COLS), BF16),
        pltpu.VMEM((ROWS, COLS), BF16),
        pltpu.VMEM((CHUNKS, ROWS, COLS), BF16),
        pltpu.VMEM((UNITS, 2, 256, COLS), BF16),
        pltpu.VMEM((UNITS, 2, 256, COLS), BF16),
        pltpu.VMEM((UNITS, 3, 2, 64, COLS), BF16),
        pltpu.VMEM((UNITS, 3, 2, 64, COLS), BF16),
        pltpu.VMEM((UNITS, 2, 64, COLS), F32),
        pltpu.VMEM((UNITS, 3, 2, 16, COLS), BF16),
        pltpu.VMEM((UNITS, 3, 2, 16, COLS), BF16),
        pltpu.VMEM((UNITS, 2, 16, COLS), F32),
        pltpu.VMEM((UNITS, 3, 8, COLS), F32),
        dma((7,)), dma((2,)), dma((CHUNKS,)), dma((CHUNKS,)), dma((CHUNKS,)),
        dma((3,)), dma((PIECES,)), dma((PIECES,)), dma((PIECES,)),
        dma((UNITS,)), dma((UNITS,)),
        dma((UNITS, 3)), dma((UNITS, 3)), dma((UNITS, 3)), dma((UNITS, 3)),
        dma((UNITS, 3)), dma((UNITS, 3)),
    ]
    return pl.pallas_call(
        kernel,
        out_shape=(
            jax.ShapeDtypeStruct((ROWS, DIM), BF16),
            jax.ShapeDtypeStruct((8, DIM), F32),
            jax.ShapeDtypeStruct((8, DIM), F32),
        ),
        in_specs=[pl.BlockSpec(memory_space=pltpu.SMEM)] + [any_space] * 5,
        out_specs=(any_space, vmem, vmem),
        scratch_shapes=scratch,
        compiler_params=pltpu.CompilerParams(
            collective_id=0, has_side_effects=True, vmem_limit_bytes=62 * 1024 * 1024),
        cost_estimate=pl.CostEstimate(
            flops=20_000_000_000, bytes_accessed=20_000_000, transcendentals=1_000_000),
    )(inv, features, tiles, w_self, w_neigh, cotangent)


def slot_of(slots):
    b = lax.axis_index("blk")
    g = lax.axis_index("grp")
    flip = g + 1 - 2 * (g % 2)
    other = (g - 1 + 2 * (g % 2)) % N_GRP
    devices = jnp.stack([
        b * N_GRP + g, (b + 1 - 2 * (b % 2)) * N_GRP + g, (3 - b) * N_GRP + g,
        b * N_GRP + flip, b * N_GRP + other])
    wanted = (devices[:, None] * BLOCKS + jnp.arange(BLOCKS)[None, :]).reshape(-1)
    match = slots[:, None, :] == wanted[None, :, None]
    place = jnp.arange(SLOTS, dtype=jnp.int32)[None, None, :]
    return jnp.min(jnp.where(match, place, SLOTS), axis=2).astype(jnp.int32)


def on_device(features, tiles, slots, w_self, w_neigh, cotangent):
    return fused(slot_of(slots), features, tiles, w_self, w_neigh, cotangent)


def solution(mesh):
    in_specs = (
        P(("blk", "grp"), None),
        P(("blk", "grp"), None, None, None),
        P(("blk", "grp"), None),
        P(),
        P(),
        P(("blk", "grp"), None),
    )
    out_specs = (P(("blk", "grp"), None), P(("blk", "grp"), None), P(("blk", "grp"), None))
    return jax.shard_map(
        on_device, mesh=mesh, in_specs=in_specs, out_specs=out_specs, check_vma=False
    )
```

```python
import functools

import jax
import jax.numpy as jnp
from jax import lax
from jax.experimental import pallas as pl
from jax.experimental.pallas import tpu as pltpu
from jax.sharding import PartitionSpec as P

MESH = pl.DeviceIdType.MESH
BLOCK = 128
SLOTS = 24
ROWS = 1024
DIM = 1024
COLS = 256
CHUNKS = DIM // COLS
BLOCKS = ROWS // BLOCK
N_GRP = 32
PIECES = CHUNKS * BLOCKS
AHEAD = 8
LAG = 3
UNITS = 2 * CHUNKS
F32 = jnp.float32
BF16 = jnp.bfloat16


def loop(count, body):
    lax.fori_loop(0, count, lambda i, _: (body(i), None)[1], None)


def kernel(
    slots_ref, feat_ref, tiles_ref, ws_ref, wn_ref, cot_ref,
    hidden_ref, gs_ref, gn_ref,
    src, adj, tbuf_even, tbuf_odd, ws, wn, cot, pre, total, left_self, left_neigh, mean, mean_in,
    rinv, table, inv_ref, dcat, hid, s1_out, s1_in, acc1, s2_out, s2_in, acc2, s3_in,
    local_sem, tile_sem, hid_sem, fc_sem, fc_recv, f_send, f1_recv, f2_recv, f3_recv,
    m_send, m_recv, dp_send, dp_recv, rs_send, s1_recv, s2_recv, s3_recv,
):
    b = lax.axis_index("blk")
    g = lax.axis_index("grp")
    z_lo = b // 2
    core = b % 2
    z_hi = g % 2
    y = (g // 2) % 4
    x = g // 8

    def at(bb, gg):
        return (bb, gg)

    core_peer = at(z_lo * 2 + (1 - core), g)
    z_peer = at(3 - b, g)
    hi_peer = at(3 - b, z_hi * (g - 1) + (1 - z_hi) * (g + 1))
    step = 2 - 4 * z_hi
    out_peer = at(b, (g + step + N_GRP) % N_GRP)
    in_peer = at(b, (g - step + N_GRP) % N_GRP)

    def x_peer(d):
        return at(b, ((x + d) % 4) * 8 + y * 2 + z_hi)

    def y_peer(d):
        return at(b, x * 8 + ((y + d) % 4) * 2 + z_hi)

    def z_ring(d):
        lo = (z_lo + d % 2) % 2
        hi = (z_hi + d // 2) % 2
        return lo, hi

    def z_dev(d):
        lo, hi = z_ring(d)
        return at(lo * 2 + core, x * 8 + y * 2 + hi)

    peers = [core_peer, z_peer, hi_peer, out_peer, in_peer]
    for d in (1, 2, 3):
        peers += [x_peer(d), y_peer(d), z_dev(d)]

    def feat_copy(c):
        return pltpu.make_async_copy(
            feat_ref.at[:, pl.ds(c * COLS, COLS)], src.at[0, c], local_sem.at[c])

    tile_bufs = (tbuf_even, tbuf_odd)

    def tile_copy(r, slot):
        return pltpu.make_async_copy(
            tiles_ref.at[r], tile_bufs[slot].at[pl.ds(0, SLOTS)], tile_sem.at[slot])

    ws_copy = pltpu.make_async_copy(ws_ref, ws, local_sem.at[4])
    wn_copy = pltpu.make_async_copy(wn_ref, wn, local_sem.at[5])
    cot_copy = pltpu.make_async_copy(cot_ref, cot, local_sem.at[6])

    barrier = pltpu.get_barrier_semaphore()
    for p in peers:
        pl.semaphore_signal(barrier, inc=1, device_id=p, device_id_type=MESH)
    tile_copy(0, 0).start()
    for c in range(CHUNKS):
        feat_copy(c).start()
    pl.semaphore_wait(barrier, len(peers))

    def piece(p):
        return p // BLOCKS, pl.ds(pl.multiple_of((p % BLOCKS) * BLOCK, BLOCK), BLOCK)

    def f1(p):
        c, rows = piece(p)
        return pltpu.make_async_remote_copy(
            src_ref=feat_ref.at[rows, pl.ds(pl.multiple_of(c * COLS, COLS), COLS)],
            dst_ref=src.at[2, c, rows],
            send_sem=f_send.at[0], recv_sem=f1_recv.at[p],
            device_id=z_peer, device_id_type=MESH)

    def f2(p):
        c, rows = piece(p)
        return pltpu.make_async_remote_copy(
            src_ref=src.at[2, c, rows], dst_ref=src.at[3, c, rows],
            send_sem=f_send.at[1], recv_sem=f2_recv.at[p],
            device_id=hi_peer, device_id_type=MESH)

    def f3(p):
        c, rows = piece(p)
        return pltpu.make_async_remote_copy(
            src_ref=src.at[3, c, rows], dst_ref=src.at[4, c, rows],
            send_sem=f_send.at[2], recv_sem=f3_recv.at[p],
            device_id=out_peer, device_id_type=MESH)

    def fc(c):
        return pltpu.make_async_remote_copy(
            src_ref=feat_ref.at[:, pl.ds(pl.multiple_of(c * COLS, COLS), COLS)],
            dst_ref=src.at[1, c],
            send_sem=fc_sem.at[c], recv_sem=fc_recv.at[c],
            device_id=core_peer, device_id_type=MESH)

    for p in range(AHEAD):
        f1(p).start()
    fc(0).start()
    ws_copy.start()
    zero_tile = jnp.zeros((BLOCK, BLOCK), BF16)
    tbuf_even[SLOTS] = zero_tile
    tbuf_odd[SLOTS] = zero_tile

    def find_slots():
        here = b * N_GRP + g
        devices = (here, here + (1 - 2 * core) * N_GRP, (3 - b) * N_GRP + g,
                   here + 1 - 2 * z_hi, b * N_GRP + (g - 1 + 2 * z_hi + N_GRP) % N_GRP)
        named = slots_ref[...]
        owner = named // BLOCKS
        column = jnp.full(named.shape, BLOCK, jnp.int32)
        for s, device in enumerate(devices):
            column = jnp.where(owner == device, s * BLOCKS + named % BLOCKS, column)
        lane = lax.broadcasted_iota(jnp.int32, (BLOCKS, BLOCK), 1)
        found = jnp.full((BLOCKS, BLOCK), SLOTS, jnp.int32)
        for k in reversed(range(SLOTS)):
            found = jnp.where(column[:, k:k + 1] == lane, k, found)
        table[...] = found
        copy = pltpu.make_async_copy(table, inv_ref, local_sem.at[7])
        copy.start()
        copy.wait()

    def build(r, slot):
        tbuf = tile_bufs[slot]

        @pl.when(r + 1 < BLOCKS)
        def _():
            tile_copy(r + 1, 1 - slot).start()

        tile_copy(r, slot).wait()
        rows = pl.ds(pl.multiple_of(r * BLOCK, BLOCK), BLOCK)

        def add(k, acc):
            for n in range(4):
                acc = acc + tbuf[4 * k + n].astype(F32)
            return acc

        deg = lax.fori_loop(0, SLOTS // 4, add, jnp.zeros((BLOCK, BLOCK), F32))
        deg = jnp.sum(deg, axis=1, keepdims=True)
        rinv[rows, :] = jnp.broadcast_to(1.0 / deg, (BLOCK, BLOCK))

        def place(s):
            for j in range(BLOCKS):
                k = inv_ref[r, s * BLOCKS + j]
                adj[s, rows, j * BLOCK:(j + 1) * BLOCK] = tbuf[k]

        loop(5, place)

    def product(s, c, first):
        part = jnp.dot(adj[s], src[s, c], preferred_element_type=F32)
        if first:
            total[c] = part
        else:
            total[c] += part

    def chunk(c):
        return pl.ds(pl.multiple_of(c * COLS, COLS), COLS)

    def pre_self(c):
        part = jnp.dot(src[0, c], ws[chunk(c), :], preferred_element_type=F32)
        for q in range(CHUNKS):
            @pl.when(c == 0)
            def _():
                pre[q] = part[:, q * COLS:(q + 1) * COLS]

            @pl.when(c > 0)
            def _():
                pre[q] += part[:, q * COLS:(q + 1) * COLS]

    def pre_neigh(c):
        part = jnp.dot(mean[c], wn[chunk(c), :], preferred_element_type=F32)
        for q in range(CHUNKS):
            pre[q] += part[:, q * COLS:(q + 1) * COLS]

    def half(lo):
        return slice(lo * COLS, (lo + 1) * COLS)

    def flip_self(lo):
        left_self[half(lo), :ROWS] = src[0, 2 * lo + core].T

    def flip_self_partner(lo):
        left_self[half(lo), ROWS:] = src[1, 2 * lo + core].T

    def flip_neigh(lo):
        left_neigh[half(lo), :ROWS] = mean[2 * lo + core].T

    def mean_copy(lo):
        return pltpu.make_async_remote_copy(
            src_ref=mean.at[2 * lo + 1 - core], dst_ref=mean_in.at[lo],
            send_sem=m_send.at[lo], recv_sem=m_recv.at[lo],
            device_id=core_peer, device_id_type=MESH)

    def flip_neigh_partner(lo):
        mean_copy(lo).wait_recv()
        left_neigh[half(lo), ROWS:] = mean_in[lo].T

    def average(c):
        def scale(m):
            rows = pl.ds(pl.multiple_of(m * 256, 256), 256)
            r = rinv[rows, :]
            value = (total[c, rows, :] * jnp.concatenate([r, r], axis=1)).astype(BF16)
            mean[c, rows, :] = value
        loop(4, scale)

        @pl.when(c % 2 != core)
        def _():
            mean_copy(c // 2).start()

    def tick(t):
        @pl.when(t < PIECES)
        def _():
            f1(t).wait_recv()
            f2(t).start()

        @pl.when(t + AHEAD < PIECES)
        def _():
            f1(t + AHEAD).start()

        @pl.when((t >= LAG) & (t < PIECES + LAG))
        def _():
            f2(t - LAG).wait_recv()
            f3(t - LAG).start()

        @pl.when(t >= 2 * LAG)
        def _():
            f3(t - 2 * LAG).wait_recv()

        phase = t // 8
        i = t % 8

        @pl.when((t < 6) & (t % 2 == 0))
        def _():
            build(t + 2, 0)

        @pl.when((t < 6) & (t % 2 == 1))
        def _():
            build(t + 2, 1)

        @pl.when((t == 6) | ((t >= 8) & (t < PIECES) & (i == 1)))
        def _():
            product(0, phase, True)

        @pl.when((t == 7) | ((t >= 8) & (t < PIECES) & (i == 4)))
        def _():
            fc(phase).wait_recv()
            product(1, phase, False)

        @pl.when((t >= 8) & ((i == 0) | (i == 3) | (i == 5)))
        def _():
            product(2 + i // 2, phase - 1, False)

        @pl.when((t >= 4) & (t < PIECES - 8) & (i == 4))
        def _():
            fc(phase + 1).start()

        @pl.when(t == 6)
        def _():
            wn_copy.start()

        @pl.when(t == 10)
        def _():
            ws_copy.wait()

        @pl.when(((t >= 8) & (t < PIECES) & (i == 2)) | (t == 36))
        def _():
            pre_self(phase - 1)

        @pl.when(t == 10)
        def _():
            flip_self(0)

        @pl.when(t == 18)
        def _():
            flip_self(1)
            flip_self_partner(0)

        @pl.when(t == 20)
        def _():
            cot_copy.start()

        @pl.when(t == 33)
        def _():
            flip_self_partner(1)

        @pl.when(t == 34)
        def _():
            flip_neigh(0)
            flip_neigh_partner(0)

        @pl.when((t >= 8) & (t < PIECES) & (i == 6))
        def _():
            average(phase - 1)

        @pl.when((t >= 8) & (t < PIECES) & (i == 7))
        def _():
            @pl.when(t == 15)
            def _():
                wn_copy.wait()

            pre_neigh(phase - 1)

    for c in range(CHUNKS):
        feat_copy(c).wait()
    find_slots()
    build(0, 0)
    build(1, 1)
    loop(PIECES + 2 * LAG, tick)
    average(CHUNKS - 1)
    cot_copy.wait()

    c0 = 0.7978845608028654
    c1 = 0.044715

    def hid_copy(q):
        return pltpu.make_async_copy(
            hid.at[q], hidden_ref.at[:, pl.ds(pl.multiple_of(q * COLS, COLS), COLS)],
            hid_sem.at[q])

    def dp_copy(q):
        return pltpu.make_async_remote_copy(
            src_ref=dcat.at[q, pl.ds(0, ROWS)], dst_ref=dcat.at[q, pl.ds(ROWS, ROWS)],
            send_sem=dp_send.at[q], recv_sem=dp_recv.at[q],
            device_id=core_peer, device_id_type=MESH)

    def gelu(q):
        pre[q] += jnp.dot(
            mean[CHUNKS - 1], wn[DIM - COLS:, q * COLS:(q + 1) * COLS], preferred_element_type=F32)
        for m in range(16):
            rows = slice(m * 64, m * 64 + 64)
            v = pre[q, rows, :]
            v2 = v * v
            th = jnp.tanh(c0 * (v + c1 * (v2 * v)))
            upper = 0.5 * (1.0 + th)
            hid[q, rows, :] = (v * upper).astype(BF16)
            slope = upper + (0.5 * v) * (1.0 - th * th) * (c0 + (3.0 * c0 * c1) * v2)
            given = cot[rows, q * COLS:(q + 1) * COLS].astype(F32)
            dcat[q, rows, :] = (given * slope).astype(BF16)
        dp_copy(q).start()
        hid_copy(q).start()

    FIRST = "xyzxyzxy"

    def peer(axis, d):
        return {"x": x_peer, "y": y_peer, "z": z_dev}[axis](d)

    def kept(u, first, count):
        return total[u // 2, pl.ds(pl.multiple_of((u % 2) * 512 + first, 8), count), :]

    def share(u, d):
        axis = FIRST[u]
        if axis == "x":
            pos = (x + d) % 4
            return jnp.concatenate([kept(u, lo * 256 + pos * 64, 64) for lo in range(2)], axis=0)
        if axis == "y":
            pos = (y + d) % 4
            return jnp.concatenate(
                [kept(u, lo * 256 + xx * 64 + pos * 16, 16) for lo in range(2) for xx in range(4)],
                axis=0)
        lo, hi = z_ring(d)
        return jnp.concatenate(
            [kept(u, lo * 256 + k * 16 + hi * 8, 8) for k in range(16)], axis=0)

    def s1(u, d):
        return pltpu.make_async_remote_copy(
            src_ref=s1_out.at[u, d - 1], dst_ref=s1_in.at[u, d - 1],
            send_sem=rs_send.at[0], recv_sem=s1_recv.at[u, d - 1],
            device_id=peer(FIRST[u], d), device_id_type=MESH)

    def second(u):
        return {"x": "y", "y": "x", "z": "x"}[FIRST[u]]

    def third(u):
        return {"x": "z", "y": "z", "z": "y"}[FIRST[u]]

    def place(axis, d):
        if axis == "z":
            lo, hi = z_ring(d)
            return lo * 2 + hi
        return ((x if axis == "x" else y) + d) % 4

    def s2(u, d):
        return pltpu.make_async_remote_copy(
            src_ref=s2_out.at[u, d - 1], dst_ref=s2_in.at[u, d - 1],
            send_sem=rs_send.at[1], recv_sem=s2_recv.at[u, d - 1],
            device_id=peer(second(u), d), device_id_type=MESH)

    def s3(u, d):
        return pltpu.make_async_remote_copy(
            src_ref=acc2.at[u, pl.ds(pl.multiple_of(place(third(u), d) * 8, 8), 8)],
            dst_ref=s3_in.at[u, d - 1],
            send_sem=rs_send.at[2], recv_sem=s3_recv.at[u, d - 1],
            device_id=peer(third(u), d), device_id_type=MESH)

    def gradient(q, kind):
        left = left_self if kind == 0 else left_neigh
        total[q, kind * 512:kind * 512 + 512, :] = jnp.dot(
            left[...], dcat[q], preferred_element_type=F32)

    def stage1(u):
        for d in (1, 2, 3):
            s1_out[u, d - 1] = share(u, d).astype(BF16)
            s1(u, d).start()

    def part2(u, d):
        pos = place(second(u), d)
        if FIRST[u] == "z":
            return acc1[u, pl.ds(pl.multiple_of(pos * 32, 32), 32), :]
        return jnp.concatenate(
            [acc1[u, pl.ds(pl.multiple_of(lo * 64 + pos * 16, 16), 16), :] for lo in range(2)], axis=0)

    def stage2(u):
        acc = share(u, 0)
        for d in (1, 2, 3):
            s1(u, d).wait_recv()
            acc = acc + s1_in[u, d - 1].astype(F32)
        acc1[u] = acc
        for d in (1, 2, 3):
            s2_out[u, d - 1] = part2(u, d).astype(BF16)
            s2(u, d).start()

    def stage3(u):
        acc = part2(u, 0)
        for d in (1, 2, 3):
            s2(u, d).wait_recv()
            acc = acc + s2_in[u, d - 1].astype(F32)
        acc2[u] = acc
        for d in (1, 2, 3):
            s3(u, d).start()

    def stage4(u):
        out = gs_ref if u % 2 == 0 else gn_ref
        acc = acc2[u, pl.ds(pl.multiple_of(place(third(u), 0) * 8, 8), 8), :]
        for d in (1, 2, 3):
            s3(u, d).wait_recv()
            acc = acc + s3_in[u, d - 1]
        out[:, (u // 2) * COLS:(u // 2 + 1) * COLS] = acc

    gelu(0)
    gelu(1)
    flip_neigh(1)
    for q in range(CHUNKS):
        if 0 < q < CHUNKS - 1:
            gelu(q + 1)
        dp_copy(q).wait_recv()
        gradient(q, 0)
        stage1(2 * q)
        if q == 0:
            flip_neigh_partner(1)
        gradient(q, 1)
        stage1(2 * q + 1)
        if q == 2:
            stage2(0)
            stage2(1)
    for u in (2, 3, 4):
        stage2(u)
    stage3(0)
    stage3(1)
    stage2(5)
    stage3(2)
    stage3(3)
    stage2(6)
    stage2(7)
    for u in (4, 5, 6, 7):
        stage3(u)
    for u in range(UNITS):
        stage4(u)

    for i in range(3):
        pltpu.make_async_copy(src.at[i + 2], src.at[i + 2], f_send.at[i]).wait()
    for i, whole in enumerate((s1_out, s2_out, s3_in)):
        pltpu.make_async_copy(whole, whole, rs_send.at[i]).wait()
    for lo in range(2):
        mean_copy(lo).wait_send()
    for q in range(CHUNKS):
        fc(q).wait_send()
        dp_copy(q).wait_send()
        hid_copy(q).wait()


def fused(slots, features, tiles, w_self, w_neigh, cotangent):
    any_space = pl.BlockSpec(memory_space=pl.ANY)
    vmem = pl.BlockSpec(memory_space=pltpu.VMEM)
    dma = pltpu.SemaphoreType.DMA
    scratch = [
        pltpu.VMEM((5, CHUNKS, ROWS, COLS), BF16),
        pltpu.VMEM((5, ROWS, ROWS), BF16),
        pltpu.VMEM((SLOTS + 1, BLOCK, BLOCK), BF16),
        pltpu.VMEM((SLOTS + 1, BLOCK, BLOCK), BF16),
        pltpu.VMEM((DIM, DIM), BF16),
        pltpu.VMEM((DIM, DIM), BF16),
        pltpu.VMEM((ROWS, DIM), BF16),
        pltpu.VMEM((CHUNKS, ROWS, COLS), F32),
        pltpu.VMEM((CHUNKS, ROWS, COLS), F32),
        pltpu.VMEM((DIM // 2, 2 * ROWS), BF16),
        pltpu.VMEM((DIM // 2, 2 * ROWS), BF16),
        pltpu.VMEM((CHUNKS, ROWS, COLS), BF16),
        pltpu.VMEM((2, ROWS, COLS), BF16),
        pltpu.VMEM((ROWS, BLOCK), F32),
        pltpu.VMEM((BLOCKS, BLOCK), jnp.int32),
        pltpu.SMEM((BLOCKS, BLOCK), jnp.int32),
        pltpu.VMEM((CHUNKS, 2 * ROWS, COLS), BF16),
        pltpu.VMEM((CHUNKS, ROWS, COLS), BF16),
        pltpu.VMEM((UNITS, 3, 128, COLS), BF16),
        pltpu.VMEM((UNITS, 3, 128, COLS), BF16),
        pltpu.VMEM((UNITS, 128, COLS), F32),
        pltpu.VMEM((UNITS, 3, 32, COLS), BF16),
        pltpu.VMEM((UNITS, 3, 32, COLS), BF16),
        pltpu.VMEM((UNITS, 32, COLS), F32),
        pltpu.VMEM((UNITS, 3, 8, COLS), F32),
        dma((8,)), dma((2,)), dma((CHUNKS,)), dma((CHUNKS,)), dma((CHUNKS,)),
        dma((3,)), dma((PIECES,)), dma((PIECES,)), dma((PIECES,)),
        dma((2,)), dma((2,)), dma((CHUNKS,)), dma((CHUNKS,)), dma((3,)),
        dma((UNITS, 3)), dma((UNITS, 3)), dma((UNITS, 3)),
    ]
    return pl.pallas_call(
        kernel,
        out_shape=(
            jax.ShapeDtypeStruct((ROWS, DIM), BF16),
            jax.ShapeDtypeStruct((8, DIM), F32),
            jax.ShapeDtypeStruct((8, DIM), F32),
        ),
        in_specs=[vmem] + [any_space] * 5,
        out_specs=(any_space, vmem, vmem),
        scratch_shapes=scratch,
        compiler_params=pltpu.CompilerParams(
            collective_id=0, has_side_effects=True, vmem_limit_bytes=62 * 1024 * 1024),
        cost_estimate=pl.CostEstimate(
            flops=20_000_000_000, bytes_accessed=20_000_000, transcendentals=1_000_000),
    )(slots, features, tiles, w_self, w_neigh, cotangent)


def settle_kernel(hid_ref, gs_ref, gn_ref, hid_out, gs_out, gn_out, buf, gbuf, sem):
    ways = [(hid_ref.at[pl.ds(i * BLOCK, BLOCK)], buf.at[pl.ds(i * BLOCK, BLOCK)],
             hid_out.at[pl.ds(i * BLOCK, BLOCK)]) for i in range(BLOCKS)]
    ways += [(gs_ref, gbuf.at[0], gs_out), (gn_ref, gbuf.at[1], gn_out)]
    first = [pltpu.make_async_copy(a, m, sem.at[0, i]) for i, (a, m, _) in enumerate(ways)]
    last = [pltpu.make_async_copy(m, c, sem.at[1, i]) for i, (_, m, c) in enumerate(ways)]
    for copy in first:
        copy.start()
    for one, two in zip(first, last):
        one.wait()
        two.start()
    for copy in last:
        copy.wait()


def settled(hidden, grad_self, grad_neigh):
    outs = (hidden, grad_self, grad_neigh)
    return pl.pallas_call(
        settle_kernel,
        out_shape=tuple(jax.ShapeDtypeStruct(a.shape, a.dtype) for a in outs),
        in_specs=[pl.BlockSpec(memory_space=pl.ANY)] * 3,
        out_specs=(pl.BlockSpec(memory_space=pl.ANY),) * 3,
        scratch_shapes=[
            pltpu.VMEM((ROWS, DIM), BF16), pltpu.VMEM((2, 8, DIM), F32),
            pltpu.SemaphoreType.DMA((2, BLOCKS + 2))],
        compiler_params=pltpu.CompilerParams(vmem_limit_bytes=62 * 1024 * 1024),
        cost_estimate=pl.CostEstimate(flops=0, bytes_accessed=4_300_000, transcendentals=0),
    )(*outs)


def on_device(features, tiles, slots, w_self, w_neigh, cotangent):
    return settled(*fused(slots, features, tiles, w_self, w_neigh, cotangent))


def solution(mesh):
    in_specs = (
        P(("blk", "grp"), None),
        P(("blk", "grp"), None, None, None),
        P(("blk", "grp"), None),
        P(),
        P(),
        P(("blk", "grp"), None),
    )
    out_specs = (P(("blk", "grp"), None), P(("blk", "grp"), None), P(("blk", "grp"), None))
    return jax.shard_map(
        on_device, mesh=mesh, in_specs=in_specs, out_specs=out_specs, check_vma=False
    )
```

```python
import functools

import jax
import jax.numpy as jnp
from jax import lax
from jax.experimental import pallas as pl
from jax.experimental.pallas import tpu as pltpu
from jax.sharding import PartitionSpec as P

MESH = pl.DeviceIdType.MESH
BLOCK = 128
SLOTS = 24
ROWS = 1024
DIM = 1024
COLS = 256
CHUNKS = DIM // COLS
BLOCKS = ROWS // BLOCK
N_GRP = 32
PIECES = CHUNKS * BLOCKS
AHEAD = 8
LAG = 3
UNITS = 2 * CHUNKS
F32 = jnp.float32
BF16 = jnp.bfloat16


def loop(count, body):
    lax.fori_loop(0, count, lambda i, _: (body(i), None)[1], None)


def kernel(
    slots_ref, feat_ref, tiles_ref, ws_ref, wn_ref, cot_ref,
    hidden_ref, gs_ref, gn_ref,
    src, adj, tbuf_even, tbuf_odd, ws, wn, cot, pre, total, left_self, left_neigh, mean, mean_in,
    rinv, table, inv_ref, dcat, hid, s1_out, s1_in, acc1, s2_out, s2_in, acc2, s3_in,
    local_sem, tile_sem, hid_sem, fc_sem, fc_recv, f_send, f1_recv, f2_recv, f3_recv,
    m_send, m_recv, dp_send, dp_recv, rs_send, s1_recv, s2_recv, s3_recv,
):
    b = lax.axis_index("blk")
    g = lax.axis_index("grp")
    z_lo = b // 2
    core = b % 2
    z_hi = g % 2
    y = (g // 2) % 4
    x = g // 8

    def at(bb, gg):
        return (bb, gg)

    core_peer = at(z_lo * 2 + (1 - core), g)
    z_peer = at(3 - b, g)
    hi_peer = at(3 - b, z_hi * (g - 1) + (1 - z_hi) * (g + 1))
    step = 2 - 4 * z_hi
    out_peer = at(b, (g + step + N_GRP) % N_GRP)
    in_peer = at(b, (g - step + N_GRP) % N_GRP)

    def x_peer(d):
        return at(b, ((x + d) % 4) * 8 + y * 2 + z_hi)

    def y_peer(d):
        return at(b, x * 8 + ((y + d) % 4) * 2 + z_hi)

    def z_ring(d):
        lo = (z_lo + d % 2) % 2
        hi = (z_hi + d // 2) % 2
        return lo, hi

    def z_dev(d):
        lo, hi = z_ring(d)
        return at(lo * 2 + core, x * 8 + y * 2 + hi)

    peers = [core_peer, z_peer, hi_peer, out_peer, in_peer]
    for d in (1, 2, 3):
        peers += [x_peer(d), y_peer(d), z_dev(d)]

    def feat_copy(c):
        return pltpu.make_async_copy(
            feat_ref.at[:, pl.ds(c * COLS, COLS)], src.at[0, c], local_sem.at[c])

    tile_bufs = (tbuf_even, tbuf_odd)

    def tile_copy(r, slot):
        return pltpu.make_async_copy(
            tiles_ref.at[r], tile_bufs[slot].at[pl.ds(0, SLOTS)], tile_sem.at[slot])

    ws_copy = pltpu.make_async_copy(ws_ref, ws, local_sem.at[4])
    wn_copy = pltpu.make_async_copy(wn_ref, wn, local_sem.at[5])
    cot_copy = pltpu.make_async_copy(cot_ref, cot, local_sem.at[6])

    barrier = pltpu.get_barrier_semaphore()
    for p in peers:
        pl.semaphore_signal(barrier, inc=1, device_id=p, device_id_type=MESH)
    tile_copy(0, 0).start()
    tile_copy(1, 1).start()
    for c in range(CHUNKS):
        feat_copy(c).start()
    pl.semaphore_wait(barrier, len(peers))

    def piece(p):
        return p // BLOCKS, pl.ds(pl.multiple_of((p % BLOCKS) * BLOCK, BLOCK), BLOCK)

    def f1(p):
        c, rows = piece(p)
        return pltpu.make_async_remote_copy(
            src_ref=feat_ref.at[rows, pl.ds(pl.multiple_of(c * COLS, COLS), COLS)],
            dst_ref=src.at[2, c, rows],
            send_sem=f_send.at[0], recv_sem=f1_recv.at[p],
            device_id=z_peer, device_id_type=MESH)

    def f2(p):
        c, rows = piece(p)
        return pltpu.make_async_remote_copy(
            src_ref=src.at[2, c, rows], dst_ref=src.at[3, c, rows],
            send_sem=f_send.at[1], recv_sem=f2_recv.at[p],
            device_id=hi_peer, device_id_type=MESH)

    def f3(p):
        c, rows = piece(p)
        return pltpu.make_async_remote_copy(
            src_ref=src.at[3, c, rows], dst_ref=src.at[4, c, rows],
            send_sem=f_send.at[2], recv_sem=f3_recv.at[p],
            device_id=out_peer, device_id_type=MESH)

    def fc(c):
        return pltpu.make_async_remote_copy(
            src_ref=feat_ref.at[:, pl.ds(pl.multiple_of(c * COLS, COLS), COLS)],
            dst_ref=src.at[1, c],
            send_sem=fc_sem.at[c], recv_sem=fc_recv.at[c],
            device_id=core_peer, device_id_type=MESH)

    for p in range(AHEAD):
        f1(p).start()
    fc(0).start()
    ws_copy.start()
    zero_tile = jnp.zeros((BLOCK, BLOCK), BF16)
    tbuf_even[SLOTS] = zero_tile
    tbuf_odd[SLOTS] = zero_tile

    def find_slots():
        here = b * N_GRP + g
        devices = (here, here + (1 - 2 * core) * N_GRP, (3 - b) * N_GRP + g,
                   here + 1 - 2 * z_hi, b * N_GRP + (g - 1 + 2 * z_hi + N_GRP) % N_GRP)
        named = slots_ref[...]
        owner = named // BLOCKS
        column = jnp.full(named.shape, BLOCK, jnp.int32)
        for s, device in enumerate(devices):
            column = jnp.where(owner == device, s * BLOCKS + named % BLOCKS, column)
        lane = lax.broadcasted_iota(jnp.int32, (BLOCKS, BLOCK), 1)
        found = jnp.full((BLOCKS, BLOCK), SLOTS, jnp.int32)
        for k in reversed(range(SLOTS)):
            found = jnp.where(column[:, k:k + 1] == lane, k, found)
        table[...] = found
        copy = pltpu.make_async_copy(table, inv_ref, local_sem.at[7])
        copy.start()
        copy.wait()

    def build(r, slot):
        tbuf = tile_bufs[slot]

        tile_copy(r, slot).wait()
        rows = pl.ds(pl.multiple_of(r * BLOCK, BLOCK), BLOCK)

        def add(k, acc):
            for n in range(4):
                acc = acc + tbuf[4 * k + n].astype(F32)
            return acc

        deg = lax.fori_loop(0, SLOTS // 4, add, jnp.zeros((BLOCK, BLOCK), F32))
        deg = jnp.sum(deg, axis=1, keepdims=True)
        rinv[rows, :] = jnp.broadcast_to(1.0 / deg, (BLOCK, BLOCK))

        def place(s):
            for j in range(BLOCKS):
                k = inv_ref[r, s * BLOCKS + j]
                adj[s, rows, j * BLOCK:(j + 1) * BLOCK] = tbuf[k]

        loop(5, place)

        @pl.when(r + 2 < BLOCKS)
        def _():
            tile_copy(r + 2, slot).start()

    def product(s, c, first):
        part = jnp.dot(adj[s], src[s, c], preferred_element_type=F32)
        if first:
            total[c] = part
        else:
            total[c] += part

    def chunk(c):
        return pl.ds(pl.multiple_of(c * COLS, COLS), COLS)

    def pre_self(c):
        part = jnp.dot(src[0, c], ws[chunk(c), :], preferred_element_type=F32)
        for q in range(CHUNKS):
            pre[q] += part[:, q * COLS:(q + 1) * COLS]

    def pre_neigh(c):
        part = jnp.dot(mean[c], wn[chunk(c), :], preferred_element_type=F32)
        for q in range(CHUNKS):
            @pl.when(c == 0)
            def _():
                pre[q] = part[:, q * COLS:(q + 1) * COLS]

            @pl.when(c > 0)
            def _():
                pre[q] += part[:, q * COLS:(q + 1) * COLS]

    def half(lo):
        return slice(lo * COLS, (lo + 1) * COLS)

    def flip_self(lo):
        left_self[half(lo), :ROWS] = src[0, 2 * lo + core].T

    def flip_self_partner(lo):
        left_self[half(lo), ROWS:] = src[1, 2 * lo + core].T

    def flip_neigh(lo):
        left_neigh[half(lo), :ROWS] = mean[2 * lo + core].T

    def mean_copy(lo):
        return pltpu.make_async_remote_copy(
            src_ref=mean.at[2 * lo + 1 - core], dst_ref=mean_in.at[lo],
            send_sem=m_send.at[lo], recv_sem=m_recv.at[lo],
            device_id=core_peer, device_id_type=MESH)

    def flip_neigh_partner(lo):
        mean_copy(lo).wait_recv()
        left_neigh[half(lo), ROWS:] = mean_in[lo].T

    def average(c):
        def scale(m):
            rows = pl.ds(pl.multiple_of(m * 256, 256), 256)
            r = rinv[rows, :]
            value = (total[c, rows, :] * jnp.concatenate([r, r], axis=1)).astype(BF16)
            mean[c, rows, :] = value
        loop(4, scale)

        @pl.when(c % 2 != core)
        def _():
            mean_copy(c // 2).start()

    def tick(t):
        @pl.when(t < PIECES)
        def _():
            f1(t).wait_recv()
            f2(t).start()

        @pl.when(t + AHEAD < PIECES)
        def _():
            f1(t + AHEAD).start()

        @pl.when((t >= LAG) & (t < PIECES + LAG))
        def _():
            f2(t - LAG).wait_recv()
            f3(t - LAG).start()

        @pl.when(t >= 2 * LAG)
        def _():
            f3(t - 2 * LAG).wait_recv()

        phase = t // 8
        i = t % 8

        @pl.when((t < 8) & (t % 2 == 0))
        def _():
            build(t, 0)

        @pl.when((t < 8) & (t % 2 == 1))
        def _():
            build(t, 1)

        @pl.when((t == 8) | ((t >= 8) & (t < PIECES) & (i == 1)))
        def _():
            product(0, phase - (t == 8).astype(jnp.int32), True)

        @pl.when((t == 10) | ((t >= 8) & (t < PIECES) & (i == 4)))
        def _():
            c = phase - (t == 10).astype(jnp.int32)
            fc(c).wait_recv()
            product(1, c, False)

        @pl.when((t >= 8) & (t < PIECES + 5) & ((i == 0) | (i == 3) | (i == 5)))
        def _():
            product(2 + i // 2, phase - 1, False)

        @pl.when((t == PIECES + 2) | (t == PIECES + 5))
        def _():
            rows = pl.ds(pl.multiple_of((t - PIECES - 2) // 3 * 512, 512), 512)
            total[CHUNKS - 1] += jnp.dot(
                adj[4, :, rows], src[4, CHUNKS - 1, rows, :], preferred_element_type=F32)

        @pl.when((t >= 4) & (t < PIECES - 8) & (i == 4))
        def _():
            fc(phase + 1).start()

        @pl.when(t == 6)
        def _():
            wn_copy.start()

        @pl.when(t == 12)
        def _():
            ws_copy.wait()

        @pl.when((t == 18) | (t == 26) | (t == 34) | (t == 36))
        def _():
            pre_self(phase - 2 + t // 36)

        @pl.when(t == 14)
        def _():
            flip_self(0)

        @pl.when(t == 22)
        def _():
            flip_self(1)

        @pl.when(t == 30)
        def _():
            flip_self_partner(0)

        @pl.when(t == 20)
        def _():
            cot_copy.start()

        @pl.when(t == 33)
        def _():
            flip_self_partner(1)

        @pl.when(t == 34)
        def _():
            flip_neigh(0)
            flip_neigh_partner(0)

        @pl.when((t >= 8) & (t < PIECES) & (i == 6))
        def _():
            average(phase - 1)

        @pl.when((t >= 8) & (t < PIECES) & (i == 7))
        def _():
            @pl.when(t == 15)
            def _():
                wn_copy.wait()

            pre_neigh(phase - 1)

    for c in range(CHUNKS):
        feat_copy(c).wait()
    find_slots()
    loop(PIECES + 2 * LAG, tick)
    average(CHUNKS - 1)
    cot_copy.wait()

    c0 = 0.7978845608028654
    c1 = 0.044715

    def hid_copy(q):
        return pltpu.make_async_copy(
            hid.at[q], hidden_ref.at[:, pl.ds(pl.multiple_of(q * COLS, COLS), COLS)],
            hid_sem.at[q])

    def dp_copy(q):
        return pltpu.make_async_remote_copy(
            src_ref=dcat.at[q, pl.ds(0, ROWS)], dst_ref=dcat.at[q, pl.ds(ROWS, ROWS)],
            send_sem=dp_send.at[q], recv_sem=dp_recv.at[q],
            device_id=core_peer, device_id_type=MESH)

    def gelu(q):
        pre[q] += jnp.dot(
            mean[CHUNKS - 1], wn[DIM - COLS:, q * COLS:(q + 1) * COLS], preferred_element_type=F32)
        for m in range(16):
            rows = slice(m * 64, m * 64 + 64)
            v = pre[q, rows, :]
            p = (c0 * c1) * (v * v)
            th = jnp.tanh(v * (c0 + p))
            upper = 0.5 + 0.5 * th
            out = v * upper
            hid[q, rows, :] = out.astype(BF16)
            slope = upper + out * (1.0 - th) * (c0 + 3.0 * p)
            given = cot[rows, q * COLS:(q + 1) * COLS].astype(F32)
            dcat[q, rows, :] = (given * slope).astype(BF16)
        dp_copy(q).start()
        hid_copy(q).start()

    FIRST = "xyzxyzxy"

    def peer(axis, d):
        return {"x": x_peer, "y": y_peer, "z": z_dev}[axis](d)

    def kept(u, first, count):
        return total[u // 2, pl.ds(pl.multiple_of((u % 2) * 512 + first, 8), count), :]

    def share(u, d):
        axis = FIRST[u]
        if axis == "x":
            pos = (x + d) % 4
            return jnp.concatenate([kept(u, lo * 256 + pos * 64, 64) for lo in range(2)], axis=0)
        if axis == "y":
            pos = (y + d) % 4
            return jnp.concatenate(
                [kept(u, lo * 256 + xx * 64 + pos * 16, 16) for lo in range(2) for xx in range(4)],
                axis=0)
        lo, hi = z_ring(d)
        return jnp.concatenate(
            [kept(u, lo * 256 + k * 16 + hi * 8, 8) for k in range(16)], axis=0)

    def s1(u, d):
        return pltpu.make_async_remote_copy(
            src_ref=s1_out.at[u, d - 1], dst_ref=s1_in.at[u, d - 1],
            send_sem=rs_send.at[0], recv_sem=s1_recv.at[u, d - 1],
            device_id=peer(FIRST[u], d), device_id_type=MESH)

    def second(u):
        return {"x": "y", "y": "x", "z": "x"}[FIRST[u]]

    def third(u):
        return {"x": "z", "y": "z", "z": "y"}[FIRST[u]]

    def place(axis, d):
        if axis == "z":
            lo, hi = z_ring(d)
            return lo * 2 + hi
        return ((x if axis == "x" else y) + d) % 4

    def s2(u, d):
        return pltpu.make_async_remote_copy(
            src_ref=s2_out.at[u, d - 1], dst_ref=s2_in.at[u, d - 1],
            send_sem=rs_send.at[1], recv_sem=s2_recv.at[u, d - 1],
            device_id=peer(second(u), d), device_id_type=MESH)

    def s3(u, d):
        return pltpu.make_async_remote_copy(
            src_ref=acc2.at[u, pl.ds(pl.multiple_of(place(third(u), d) * 8, 8), 8)],
            dst_ref=s3_in.at[u, d - 1],
            send_sem=rs_send.at[2], recv_sem=s3_recv.at[u, d - 1],
            device_id=peer(third(u), d), device_id_type=MESH)

    def gradient(q, kind):
        left = left_self if kind == 0 else left_neigh
        total[q, kind * 512:kind * 512 + 512, :] = jnp.dot(
            left[...], dcat[q], preferred_element_type=F32)

    def stage1(u):
        for d in (1, 2, 3):
            s1_out[u, d - 1] = share(u, d).astype(BF16)
            s1(u, d).start()

    def part2(u, d):
        pos = place(second(u), d)
        if FIRST[u] == "z":
            return acc1[u, pl.ds(pl.multiple_of(pos * 32, 32), 32), :]
        return jnp.concatenate(
            [acc1[u, pl.ds(pl.multiple_of(lo * 64 + pos * 16, 16), 16), :] for lo in range(2)], axis=0)

    def stage2(u):
        acc = share(u, 0)
        for d in (1, 2, 3):
            s1(u, d).wait_recv()
            acc = acc + s1_in[u, d - 1].astype(F32)
        acc1[u] = acc
        for d in (1, 2, 3):
            s2_out[u, d - 1] = part2(u, d).astype(BF16)
            s2(u, d).start()

    def stage3(u):
        acc = part2(u, 0)
        for d in (1, 2, 3):
            s2(u, d).wait_recv()
            acc = acc + s2_in[u, d - 1].astype(F32)
        acc2[u] = acc
        for d in (1, 2, 3):
            s3(u, d).start()

    def stage4(u):
        out = gs_ref if u % 2 == 0 else gn_ref
        acc = acc2[u, pl.ds(pl.multiple_of(place(third(u), 0) * 8, 8), 8), :]
        for d in (1, 2, 3):
            s3(u, d).wait_recv()
            acc = acc + s3_in[u, d - 1]
        out[:, (u // 2) * COLS:(u // 2 + 1) * COLS] = acc

    gelu(0)
    gelu(1)
    flip_neigh(1)
    for q in range(CHUNKS):
        if 0 < q < CHUNKS - 1:
            gelu(q + 1)
        dp_copy(q).wait_recv()
        gradient(q, 0)
        stage1(2 * q)
        if q == 0:
            flip_neigh_partner(1)
        gradient(q, 1)
        stage1(2 * q + 1)
        if q == 2:
            stage2(0)
            stage2(1)
    for u in (2, 3, 4):
        stage2(u)
    stage3(0)
    stage3(1)
    for u in (5, 6, 7):
        stage2(u)
    for u in range(2, UNITS):
        stage3(u)
    for u in range(UNITS):
        stage4(u)

    for i in range(3):
        pltpu.make_async_copy(src.at[i + 2], src.at[i + 2], f_send.at[i]).wait()
    for i, whole in enumerate((s1_out, s2_out, s3_in)):
        pltpu.make_async_copy(whole, whole, rs_send.at[i]).wait()
    for lo in range(2):
        mean_copy(lo).wait_send()
    for q in range(CHUNKS):
        fc(q).wait_send()
        dp_copy(q).wait_send()
        hid_copy(q).wait()


def fused(slots, features, tiles, w_self, w_neigh, cotangent):
    any_space = pl.BlockSpec(memory_space=pl.ANY)
    vmem = pl.BlockSpec(memory_space=pltpu.VMEM)
    dma = pltpu.SemaphoreType.DMA
    scratch = [
        pltpu.VMEM((5, CHUNKS, ROWS, COLS), BF16),
        pltpu.VMEM((5, ROWS, ROWS), BF16),
        pltpu.VMEM((SLOTS + 1, BLOCK, BLOCK), BF16),
        pltpu.VMEM((SLOTS + 1, BLOCK, BLOCK), BF16),
        pltpu.VMEM((DIM, DIM), BF16),
        pltpu.VMEM((DIM, DIM), BF16),
        pltpu.VMEM((ROWS, DIM), BF16),
        pltpu.VMEM((CHUNKS, ROWS, COLS), F32),
        pltpu.VMEM((CHUNKS, ROWS, COLS), F32),
        pltpu.VMEM((DIM // 2, 2 * ROWS), BF16),
        pltpu.VMEM((DIM // 2, 2 * ROWS), BF16),
        pltpu.VMEM((CHUNKS, ROWS, COLS), BF16),
        pltpu.VMEM((2, ROWS, COLS), BF16),
        pltpu.VMEM((ROWS, BLOCK), F32),
        pltpu.VMEM((BLOCKS, BLOCK), jnp.int32),
        pltpu.SMEM((BLOCKS, BLOCK), jnp.int32),
        pltpu.VMEM((CHUNKS, 2 * ROWS, COLS), BF16),
        pltpu.VMEM((CHUNKS, ROWS, COLS), BF16),
        pltpu.VMEM((UNITS, 3, 128, COLS), BF16),
        pltpu.VMEM((UNITS, 3, 128, COLS), BF16),
        pltpu.VMEM((UNITS, 128, COLS), F32),
        pltpu.VMEM((UNITS, 3, 32, COLS), BF16),
        pltpu.VMEM((UNITS, 3, 32, COLS), BF16),
        pltpu.VMEM((UNITS, 32, COLS), F32),
        pltpu.VMEM((UNITS, 3, 8, COLS), F32),
        dma((8,)), dma((2,)), dma((CHUNKS,)), dma((CHUNKS,)), dma((CHUNKS,)),
        dma((3,)), dma((PIECES,)), dma((PIECES,)), dma((PIECES,)),
        dma((2,)), dma((2,)), dma((CHUNKS,)), dma((CHUNKS,)), dma((3,)),
        dma((UNITS, 3)), dma((UNITS, 3)), dma((UNITS, 3)),
    ]
    return pl.pallas_call(
        kernel,
        out_shape=(
            jax.ShapeDtypeStruct((ROWS, DIM), BF16),
            jax.ShapeDtypeStruct((8, DIM), F32),
            jax.ShapeDtypeStruct((8, DIM), F32),
        ),
        in_specs=[vmem] + [any_space] * 5,
        out_specs=(any_space, vmem, vmem),
        scratch_shapes=scratch,
        compiler_params=pltpu.CompilerParams(
            collective_id=0, has_side_effects=True, vmem_limit_bytes=62 * 1024 * 1024),
        cost_estimate=pl.CostEstimate(
            flops=20_000_000_000, bytes_accessed=20_000_000, transcendentals=1_000_000),
    )(slots, features, tiles, w_self, w_neigh, cotangent)


def settle_kernel(hid_ref, gs_ref, gn_ref, hid_out, gs_out, gn_out, buf, gbuf, sem):
    ways = [(hid_ref.at[pl.ds(i * BLOCK, BLOCK)], buf.at[pl.ds(i * BLOCK, BLOCK)],
             hid_out.at[pl.ds(i * BLOCK, BLOCK)]) for i in range(BLOCKS)]
    ways += [(gs_ref, gbuf.at[0], gs_out), (gn_ref, gbuf.at[1], gn_out)]
    first = [pltpu.make_async_copy(a, m, sem.at[0, i]) for i, (a, m, _) in enumerate(ways)]
    last = [pltpu.make_async_copy(m, c, sem.at[1, i]) for i, (_, m, c) in enumerate(ways)]
    for copy in first:
        copy.start()
    for one, two in zip(first, last):
        one.wait()
        two.start()
    for copy in last:
        copy.wait()


def settled(hidden, grad_self, grad_neigh):
    outs = (hidden, grad_self, grad_neigh)
    return pl.pallas_call(
        settle_kernel,
        out_shape=tuple(jax.ShapeDtypeStruct(a.shape, a.dtype) for a in outs),
        in_specs=[pl.BlockSpec(memory_space=pl.ANY)] * 3,
        out_specs=(pl.BlockSpec(memory_space=pl.ANY),) * 3,
        scratch_shapes=[
            pltpu.VMEM((ROWS, DIM), BF16), pltpu.VMEM((2, 8, DIM), F32),
            pltpu.SemaphoreType.DMA((2, BLOCKS + 2))],
        compiler_params=pltpu.CompilerParams(vmem_limit_bytes=62 * 1024 * 1024),
        cost_estimate=pl.CostEstimate(flops=0, bytes_accessed=4_300_000, transcendentals=0),
    )(*outs)


def on_device(features, tiles, slots, w_self, w_neigh, cotangent):
    return settled(*fused(slots, features, tiles, w_self, w_neigh, cotangent))


def solution(mesh):
    in_specs = (
        P(("blk", "grp"), None),
        P(("blk", "grp"), None, None, None),
        P(("blk", "grp"), None),
        P(),
        P(),
        P(("blk", "grp"), None),
    )
    out_specs = (P(("blk", "grp"), None), P(("blk", "grp"), None), P(("blk", "grp"), None))
    return jax.shard_map(
        on_device, mesh=mesh, in_specs=in_specs, out_specs=out_specs, check_vma=False
    )
```

```python
import functools

import jax
import jax.numpy as jnp
from jax import lax
from jax.experimental import pallas as pl
from jax.experimental.pallas import tpu as pltpu
from jax.sharding import PartitionSpec as P

MESH = pl.DeviceIdType.MESH
BLOCK = 128
SLOTS = 24
ROWS = 1024
DIM = 1024
COLS = 256
CHUNKS = DIM // COLS
BLOCKS = ROWS // BLOCK
N_GRP = 32
PIECES = CHUNKS * BLOCKS
AHEAD = 8
LAG = 3
UNITS = 2 * CHUNKS
F32 = jnp.float32
BF16 = jnp.bfloat16


def loop(count, body):
    lax.fori_loop(0, count, lambda i, _: (body(i), None)[1], None)


def kernel(
    slots_ref, feat_ref, tiles_ref, ws_ref, wn_ref, cot_ref,
    hidden_ref, gs_ref, gn_ref,
    src, adj, tbuf_even, tbuf_odd, ws, wn, cot, pre, total, left_self, left_neigh, mean, mean_in,
    rinv, table, inv_ref, dcat, hid, s1_out, s1_in, acc1, s2_out, s2_in, acc2, s3_in,
    local_sem, tile_sem, hid_sem, fc_sem, fc_recv, f_send, f1_recv, f2_recv, f3_recv,
    m_send, m_recv, dp_send, dp_recv, rs_send, s1_recv, s2_recv, s3_recv,
):
    b = lax.axis_index("blk")
    g = lax.axis_index("grp")
    z_lo = b // 2
    core = b % 2
    z_hi = g % 2
    y = (g // 2) % 4
    x = g // 8

    def at(bb, gg):
        return (bb, gg)

    core_peer = at(z_lo * 2 + (1 - core), g)
    z_peer = at(3 - b, g)
    hi_peer = at(3 - b, z_hi * (g - 1) + (1 - z_hi) * (g + 1))
    step = 2 - 4 * z_hi
    out_peer = at(b, (g + step + N_GRP) % N_GRP)
    in_peer = at(b, (g - step + N_GRP) % N_GRP)

    def x_peer(d):
        return at(b, ((x + d) % 4) * 8 + y * 2 + z_hi)

    def y_peer(d):
        return at(b, x * 8 + ((y + d) % 4) * 2 + z_hi)

    def z_ring(d):
        lo = (z_lo + d % 2) % 2
        hi = (z_hi + d // 2) % 2
        return lo, hi

    def z_dev(d):
        lo, hi = z_ring(d)
        return at(lo * 2 + core, x * 8 + y * 2 + hi)

    peers = [core_peer, z_peer, hi_peer, out_peer, in_peer]
    for d in (2, 1, 3):
        peers += [x_peer(d), y_peer(d), z_dev(d)]

    def feat_copy(c):
        return pltpu.make_async_copy(
            feat_ref.at[:, pl.ds(c * COLS, COLS)], src.at[0, c], local_sem.at[c])

    tile_bufs = (tbuf_even, tbuf_odd)

    def tile_copy(r, slot):
        return pltpu.make_async_copy(
            tiles_ref.at[r], tile_bufs[slot].at[pl.ds(0, SLOTS)], tile_sem.at[slot])

    ws_copy = pltpu.make_async_copy(ws_ref, ws, local_sem.at[4])
    wn_copy = pltpu.make_async_copy(wn_ref, wn, local_sem.at[5])
    cot_copy = pltpu.make_async_copy(cot_ref, cot, local_sem.at[6])

    barrier = pltpu.get_barrier_semaphore()
    for p in peers:
        pl.semaphore_signal(barrier, inc=1, device_id=p, device_id_type=MESH)
    tile_copy(0, 0).start()
    tile_copy(1, 1).start()
    for c in range(CHUNKS):
        feat_copy(c).start()
    pl.semaphore_wait(barrier, len(peers))

    def piece(p):
        return p // BLOCKS, pl.ds(pl.multiple_of((p % BLOCKS) * BLOCK, BLOCK), BLOCK)

    def f1(p):
        c, rows = piece(p)
        return pltpu.make_async_remote_copy(
            src_ref=feat_ref.at[rows, pl.ds(pl.multiple_of(c * COLS, COLS), COLS)],
            dst_ref=src.at[2, c, rows],
            send_sem=f_send.at[0], recv_sem=f1_recv.at[p],
            device_id=z_peer, device_id_type=MESH)

    def f2(p):
        c, rows = piece(p)
        return pltpu.make_async_remote_copy(
            src_ref=src.at[2, c, rows], dst_ref=src.at[3, c, rows],
            send_sem=f_send.at[1], recv_sem=f2_recv.at[p],
            device_id=hi_peer, device_id_type=MESH)

    def f3(p):
        c, rows = piece(p)
        return pltpu.make_async_remote_copy(
            src_ref=src.at[3, c, rows], dst_ref=src.at[4, c, rows],
            send_sem=f_send.at[2], recv_sem=f3_recv.at[p],
            device_id=out_peer, device_id_type=MESH)

    def fc(c):
        return pltpu.make_async_remote_copy(
            src_ref=feat_ref.at[:, pl.ds(pl.multiple_of(c * COLS, COLS), COLS)],
            dst_ref=src.at[1, c],
            send_sem=fc_sem.at[c], recv_sem=fc_recv.at[c],
            device_id=core_peer, device_id_type=MESH)

    for p in range(AHEAD):
        f1(p).start()
    fc(0).start()
    ws_copy.start()
    zero_tile = jnp.zeros((BLOCK, BLOCK), BF16)
    tbuf_even[SLOTS] = zero_tile
    tbuf_odd[SLOTS] = zero_tile

    def find_slots():
        here = b * N_GRP + g
        devices = (here, here + (1 - 2 * core) * N_GRP, (3 - b) * N_GRP + g,
                   here + 1 - 2 * z_hi, b * N_GRP + (g - 1 + 2 * z_hi + N_GRP) % N_GRP)
        named = slots_ref[...]
        owner = named // BLOCKS
        column = jnp.full(named.shape, BLOCK, jnp.int32)
        for s, device in enumerate(devices):
            column = jnp.where(owner == device, s * BLOCKS + named % BLOCKS, column)
        lane = lax.broadcasted_iota(jnp.int32, (BLOCKS, BLOCK), 1)
        found = jnp.full((BLOCKS, BLOCK), SLOTS, jnp.int32)
        for k in reversed(range(SLOTS)):
            found = jnp.where(column[:, k:k + 1] == lane, k, found)
        table[...] = found
        copy = pltpu.make_async_copy(table, inv_ref, local_sem.at[7])
        copy.start()
        copy.wait()

    def build(r, slot):
        tbuf = tile_bufs[slot]

        tile_copy(r, slot).wait()
        rows = pl.ds(pl.multiple_of(r * BLOCK, BLOCK), BLOCK)

        def add(k, acc):
            for n in range(4):
                acc = acc + tbuf[4 * k + n].astype(F32)
            return acc

        deg = lax.fori_loop(0, SLOTS // 4, add, jnp.zeros((BLOCK, BLOCK), F32))
        deg = jnp.sum(deg, axis=1, keepdims=True)
        rinv[rows, :] = jnp.broadcast_to(1.0 / deg, (BLOCK, BLOCK))

        def place(s):
            for j in range(BLOCKS):
                k = inv_ref[r, s * BLOCKS + j]
                adj[s, rows, j * BLOCK:(j + 1) * BLOCK] = tbuf[k]

        loop(5, place)

        @pl.when(r + 2 < BLOCKS)
        def _():
            tile_copy(r + 2, slot).start()

    def product(s, c, first):
        part = jnp.dot(adj[s], src[s, c], preferred_element_type=F32)
        if first:
            total[c] = part
        else:
            total[c] += part

    def chunk(c):
        return pl.ds(pl.multiple_of(c * COLS, COLS), COLS)

    def pre_self(c):
        part = jnp.dot(src[0, c], ws[chunk(c), :], preferred_element_type=F32)
        for q in range(CHUNKS):
            pre[q] += part[:, q * COLS:(q + 1) * COLS]

    def pre_neigh(c):
        part = jnp.dot(mean[c], wn[chunk(c), :], preferred_element_type=F32)
        for q in range(CHUNKS):
            @pl.when(c == 0)
            def _():
                pre[q] = part[:, q * COLS:(q + 1) * COLS]

            @pl.when(c > 0)
            def _():
                pre[q] += part[:, q * COLS:(q + 1) * COLS]

    def half(lo):
        return slice(lo * COLS, (lo + 1) * COLS)

    def flip_self(lo):
        left_self[half(lo), :ROWS] = src[0, 2 * lo + core].T

    def flip_self_partner(lo):
        left_self[half(lo), ROWS:] = src[1, 2 * lo + core].T

    def flip_neigh(lo):
        left_neigh[half(lo), :ROWS] = mean[2 * lo + core].T

    def mean_copy(lo):
        return pltpu.make_async_remote_copy(
            src_ref=mean.at[2 * lo + 1 - core], dst_ref=mean_in.at[lo],
            send_sem=m_send.at[lo], recv_sem=m_recv.at[lo],
            device_id=core_peer, device_id_type=MESH)

    def flip_neigh_partner(lo):
        mean_copy(lo).wait_recv()
        left_neigh[half(lo), ROWS:] = mean_in[lo].T

    def average(c):
        def scale(m):
            rows = pl.ds(pl.multiple_of(m * 256, 256), 256)
            r = rinv[rows, :]
            value = (total[c, rows, :] * jnp.concatenate([r, r], axis=1)).astype(BF16)
            mean[c, rows, :] = value
        loop(4, scale)

        @pl.when(c % 2 != core)
        def _():
            mean_copy(c // 2).start()

    def tick(t):
        @pl.when(t < PIECES)
        def _():
            f1(t).wait_recv()
            f2(t).start()

        @pl.when(t + AHEAD < PIECES)
        def _():
            f1(t + AHEAD).start()

        @pl.when((t >= LAG) & (t < PIECES + LAG))
        def _():
            f2(t - LAG).wait_recv()
            f3(t - LAG).start()

        @pl.when(t >= 2 * LAG)
        def _():
            f3(t - 2 * LAG).wait_recv()

        phase = t // 8
        i = t % 8

        @pl.when((t < 8) & (t % 2 == 0))
        def _():
            build(t, 0)

        @pl.when((t < 8) & (t % 2 == 1))
        def _():
            build(t, 1)

        @pl.when((t == 8) | ((t >= 8) & (t < PIECES) & (i == 1)))
        def _():
            product(0, phase - (t == 8).astype(jnp.int32), True)

        @pl.when((t == 10) | ((t >= 8) & (t < PIECES) & (i == 4)))
        def _():
            c = phase - (t == 10).astype(jnp.int32)
            fc(c).wait_recv()
            product(1, c, False)

        @pl.when((t >= 8) & (t < PIECES + 5) & ((i == 0) | (i == 3) | (i == 5)))
        def _():
            product(2 + i // 2, phase - 1, False)

        @pl.when((t == PIECES + 2) | (t == PIECES + 5))
        def _():
            rows = pl.ds(pl.multiple_of((t - PIECES - 2) // 3 * 512, 512), 512)
            total[CHUNKS - 1] += jnp.dot(
                adj[4, :, rows], src[4, CHUNKS - 1, rows, :], preferred_element_type=F32)

        @pl.when((t >= 4) & (t < PIECES - 8) & (i == 4))
        def _():
            fc(phase + 1).start()

        @pl.when(t == 6)
        def _():
            wn_copy.start()

        @pl.when(t == 12)
        def _():
            ws_copy.wait()

        @pl.when((t == 18) | (t == 26) | (t == 34) | (t == 36))
        def _():
            pre_self(phase - 2 + t // 36)

        @pl.when(t == 14)
        def _():
            flip_self(0)

        @pl.when(t == 22)
        def _():
            flip_self(1)

        @pl.when(t == 30)
        def _():
            flip_self_partner(0)

        @pl.when(t == 20)
        def _():
            cot_copy.start()

        @pl.when(t == 33)
        def _():
            flip_self_partner(1)

        @pl.when(t == 34)
        def _():
            flip_neigh(0)
            flip_neigh_partner(0)

        @pl.when((t >= 8) & (t < PIECES) & (i == 6))
        def _():
            average(phase - 1)

        @pl.when((t >= 8) & (t < PIECES) & (i == 7))
        def _():
            @pl.when(t == 15)
            def _():
                wn_copy.wait()

            pre_neigh(phase - 1)

    for c in range(CHUNKS):
        feat_copy(c).wait()
    find_slots()
    loop(PIECES + 2 * LAG, tick)
    average(CHUNKS - 1)
    cot_copy.wait()

    c0 = 0.7978845608028654
    c1 = 0.044715

    def hid_copy(q):
        return pltpu.make_async_copy(
            hid.at[q], hidden_ref.at[:, pl.ds(pl.multiple_of(q * COLS, COLS), COLS)],
            hid_sem.at[q])

    def dp_copy(q):
        return pltpu.make_async_remote_copy(
            src_ref=dcat.at[q, pl.ds(0, ROWS)], dst_ref=dcat.at[q, pl.ds(ROWS, ROWS)],
            send_sem=dp_send.at[q], recv_sem=dp_recv.at[q],
            device_id=core_peer, device_id_type=MESH)

    def gelu(q):
        pre[q] += jnp.dot(
            mean[CHUNKS - 1], wn[DIM - COLS:, q * COLS:(q + 1) * COLS], preferred_element_type=F32)
        for m in range(16):
            rows = slice(m * 64, m * 64 + 64)
            v = pre[q, rows, :]
            p = (c0 * c1) * (v * v)
            th = jnp.tanh(v * (c0 + p))
            upper = 0.5 + 0.5 * th
            out = v * upper
            hid[q, rows, :] = out.astype(BF16)
            slope = upper + out * (1.0 - th) * (c0 + 3.0 * p)
            given = cot[rows, q * COLS:(q + 1) * COLS].astype(F32)
            dcat[q, rows, :] = (given * slope).astype(BF16)
        dp_copy(q).start()
        hid_copy(q).start()

    FIRST = "xyzxyzxy"

    def peer(axis, d):
        return {"x": x_peer, "y": y_peer, "z": z_dev}[axis](d)

    def kept(u, first, count):
        return total[u // 2, pl.ds(pl.multiple_of((u % 2) * 512 + first, 8), count), :]

    def share(u, d):
        axis = FIRST[u]
        if axis == "x":
            pos = (x + d) % 4
            return jnp.concatenate([kept(u, lo * 256 + pos * 64, 64) for lo in range(2)], axis=0)
        if axis == "y":
            pos = (y + d) % 4
            return jnp.concatenate(
                [kept(u, lo * 256 + xx * 64 + pos * 16, 16) for lo in range(2) for xx in range(4)],
                axis=0)
        lo, hi = z_ring(d)
        return jnp.concatenate(
            [kept(u, lo * 256 + k * 16 + hi * 8, 8) for k in range(16)], axis=0)

    def s1(u, d):
        return pltpu.make_async_remote_copy(
            src_ref=s1_out.at[u, d - 1], dst_ref=s1_in.at[u, d - 1],
            send_sem=rs_send.at[0], recv_sem=s1_recv.at[u, d - 1],
            device_id=peer(FIRST[u], d), device_id_type=MESH)

    def second(u):
        return {"x": "y", "y": "x", "z": "x"}[FIRST[u]]

    def third(u):
        return {"x": "z", "y": "z", "z": "y"}[FIRST[u]]

    def place(axis, d):
        if axis == "z":
            lo, hi = z_ring(d)
            return lo * 2 + hi
        return ((x if axis == "x" else y) + d) % 4

    def s2(u, d):
        return pltpu.make_async_remote_copy(
            src_ref=s2_out.at[u, d - 1], dst_ref=s2_in.at[u, d - 1],
            send_sem=rs_send.at[1], recv_sem=s2_recv.at[u, d - 1],
            device_id=peer(second(u), d), device_id_type=MESH)

    def s3(u, d):
        return pltpu.make_async_remote_copy(
            src_ref=acc2.at[u, pl.ds(pl.multiple_of(place(third(u), d) * 8, 8), 8)],
            dst_ref=s3_in.at[u, d - 1],
            send_sem=rs_send.at[2], recv_sem=s3_recv.at[u, d - 1],
            device_id=peer(third(u), d), device_id_type=MESH)

    def gradient(q, kind):
        left = left_self if kind == 0 else left_neigh
        total[q, kind * 512:kind * 512 + 512, :] = jnp.dot(
            left[...], dcat[q], preferred_element_type=F32)

    def stage1(u):
        for d in (2, 1, 3):
            s1_out[u, d - 1] = share(u, d).astype(BF16)
            s1(u, d).start()

    def part2(u, d):
        pos = place(second(u), d)
        if FIRST[u] == "z":
            return acc1[u, pl.ds(pl.multiple_of(pos * 32, 32), 32), :]
        return jnp.concatenate(
            [acc1[u, pl.ds(pl.multiple_of(lo * 64 + pos * 16, 16), 16), :] for lo in range(2)], axis=0)

    def stage2(u):
        acc = share(u, 0)
        for d in (2, 1, 3):
            s1(u, d).wait_recv()
            acc = acc + s1_in[u, d - 1].astype(F32)
        acc1[u] = acc
        for d in (2, 1, 3):
            s2_out[u, d - 1] = part2(u, d).astype(BF16)
            s2(u, d).start()

    def stage3(u):
        acc = part2(u, 0)
        for d in (2, 1, 3):
            s2(u, d).wait_recv()
            acc = acc + s2_in[u, d - 1].astype(F32)
        acc2[u] = acc
        for d in (2, 1, 3):
            s3(u, d).start()

    def stage4(u):
        out = gs_ref if u % 2 == 0 else gn_ref
        acc = acc2[u, pl.ds(pl.multiple_of(place(third(u), 0) * 8, 8), 8), :]
        for d in (2, 1, 3):
            s3(u, d).wait_recv()
            acc = acc + s3_in[u, d - 1]
        out[:, (u // 2) * COLS:(u // 2 + 1) * COLS] = acc

    gelu(0)
    gelu(1)
    flip_neigh(1)
    for q in range(CHUNKS):
        if 0 < q < CHUNKS - 1:
            gelu(q + 1)
        dp_copy(q).wait_recv()
        gradient(q, 0)
        stage1(2 * q)
        if q == 0:
            flip_neigh_partner(1)
        gradient(q, 1)
        stage1(2 * q + 1)
        if q == 2:
            stage2(0)
            stage2(1)
    for u in (2, 3, 4):
        stage2(u)
    stage3(0)
    stage3(1)
    for u in (5, 6, 7):
        stage2(u)
    for u in range(2, UNITS):
        stage3(u)
    for u in range(UNITS):
        stage4(u)

    for i in range(3):
        pltpu.make_async_copy(src.at[i + 2], src.at[i + 2], f_send.at[i]).wait()
    for i, whole in enumerate((s1_out, s2_out, s3_in)):
        pltpu.make_async_copy(whole, whole, rs_send.at[i]).wait()
    for lo in range(2):
        mean_copy(lo).wait_send()
    for q in range(CHUNKS):
        fc(q).wait_send()
        dp_copy(q).wait_send()
        hid_copy(q).wait()


def fused(slots, features, tiles, w_self, w_neigh, cotangent):
    any_space = pl.BlockSpec(memory_space=pl.ANY)
    vmem = pl.BlockSpec(memory_space=pltpu.VMEM)
    dma = pltpu.SemaphoreType.DMA
    scratch = [
        pltpu.VMEM((5, CHUNKS, ROWS, COLS), BF16),
        pltpu.VMEM((5, ROWS, ROWS), BF16),
        pltpu.VMEM((SLOTS + 1, BLOCK, BLOCK), BF16),
        pltpu.VMEM((SLOTS + 1, BLOCK, BLOCK), BF16),
        pltpu.VMEM((DIM, DIM), BF16),
        pltpu.VMEM((DIM, DIM), BF16),
        pltpu.VMEM((ROWS, DIM), BF16),
        pltpu.VMEM((CHUNKS, ROWS, COLS), F32),
        pltpu.VMEM((CHUNKS, ROWS, COLS), F32),
        pltpu.VMEM((DIM // 2, 2 * ROWS), BF16),
        pltpu.VMEM((DIM // 2, 2 * ROWS), BF16),
        pltpu.VMEM((CHUNKS, ROWS, COLS), BF16),
        pltpu.VMEM((2, ROWS, COLS), BF16),
        pltpu.VMEM((ROWS, BLOCK), F32),
        pltpu.VMEM((BLOCKS, BLOCK), jnp.int32),
        pltpu.SMEM((BLOCKS, BLOCK), jnp.int32),
        pltpu.VMEM((CHUNKS, 2 * ROWS, COLS), BF16),
        pltpu.VMEM((CHUNKS, ROWS, COLS), BF16),
        pltpu.VMEM((UNITS, 3, 128, COLS), BF16),
        pltpu.VMEM((UNITS, 3, 128, COLS), BF16),
        pltpu.VMEM((UNITS, 128, COLS), F32),
        pltpu.VMEM((UNITS, 3, 32, COLS), BF16),
        pltpu.VMEM((UNITS, 3, 32, COLS), BF16),
        pltpu.VMEM((UNITS, 32, COLS), F32),
        pltpu.VMEM((UNITS, 3, 8, COLS), F32),
        dma((8,)), dma((2,)), dma((CHUNKS,)), dma((CHUNKS,)), dma((CHUNKS,)),
        dma((3,)), dma((PIECES,)), dma((PIECES,)), dma((PIECES,)),
        dma((2,)), dma((2,)), dma((CHUNKS,)), dma((CHUNKS,)), dma((3,)),
        dma((UNITS, 3)), dma((UNITS, 3)), dma((UNITS, 3)),
    ]
    return pl.pallas_call(
        kernel,
        out_shape=(
            jax.ShapeDtypeStruct((ROWS, DIM), BF16),
            jax.ShapeDtypeStruct((8, DIM), F32),
            jax.ShapeDtypeStruct((8, DIM), F32),
        ),
        in_specs=[vmem] + [any_space] * 5,
        out_specs=(any_space, vmem, vmem),
        scratch_shapes=scratch,
        compiler_params=pltpu.CompilerParams(
            collective_id=0, has_side_effects=True, vmem_limit_bytes=62 * 1024 * 1024),
        cost_estimate=pl.CostEstimate(
            flops=20_000_000_000, bytes_accessed=20_000_000, transcendentals=1_000_000),
    )(slots, features, tiles, w_self, w_neigh, cotangent)


def settle_kernel(hid_ref, gs_ref, gn_ref, hid_out, gs_out, gn_out, buf, gbuf, sem):
    ways = [(hid_ref.at[pl.ds(i * BLOCK, BLOCK)], buf.at[pl.ds(i * BLOCK, BLOCK)],
             hid_out.at[pl.ds(i * BLOCK, BLOCK)]) for i in range(BLOCKS)]
    ways += [(gs_ref, gbuf.at[0], gs_out), (gn_ref, gbuf.at[1], gn_out)]
    first = [pltpu.make_async_copy(a, m, sem.at[0, i]) for i, (a, m, _) in enumerate(ways)]
    last = [pltpu.make_async_copy(m, c, sem.at[1, i]) for i, (_, m, c) in enumerate(ways)]
    for copy in first:
        copy.start()
    for one, two in zip(first, last):
        one.wait()
        two.start()
    for copy in last:
        copy.wait()


def settled(hidden, grad_self, grad_neigh):
    outs = (hidden, grad_self, grad_neigh)
    return pl.pallas_call(
        settle_kernel,
        out_shape=tuple(jax.ShapeDtypeStruct(a.shape, a.dtype) for a in outs),
        in_specs=[pl.BlockSpec(memory_space=pl.ANY)] * 3,
        out_specs=(pl.BlockSpec(memory_space=pl.ANY),) * 3,
        scratch_shapes=[
            pltpu.VMEM((ROWS, DIM), BF16), pltpu.VMEM((2, 8, DIM), F32),
            pltpu.SemaphoreType.DMA((2, BLOCKS + 2))],
        compiler_params=pltpu.CompilerParams(vmem_limit_bytes=62 * 1024 * 1024),
        cost_estimate=pl.CostEstimate(flops=0, bytes_accessed=4_300_000, transcendentals=0),
    )(*outs)


def on_device(features, tiles, slots, w_self, w_neigh, cotangent):
    return settled(*fused(slots, features, tiles, w_self, w_neigh, cotangent))


def solution(mesh):
    in_specs = (
        P(("blk", "grp"), None),
        P(("blk", "grp"), None, None, None),
        P(("blk", "grp"), None),
        P(),
        P(),
        P(("blk", "grp"), None),
    )
    out_specs = (P(("blk", "grp"), None), P(("blk", "grp"), None), P(("blk", "grp"), None))
    return jax.shard_map(
        on_device, mesh=mesh, in_specs=in_specs, out_specs=out_specs, check_vma=False
    )
```

```python
import functools

import jax
import jax.numpy as jnp
from jax import lax
from jax.experimental import pallas as pl
from jax.experimental.pallas import tpu as pltpu
from jax.sharding import PartitionSpec as P

MESH = pl.DeviceIdType.MESH
BLOCK = 128
SLOTS = 24
ROWS = 1024
DIM = 1024
COLS = 256
CHUNKS = DIM // COLS
BLOCKS = ROWS // BLOCK
N_GRP = 32
PIECES = CHUNKS * BLOCKS
SENT = 2 * PIECES
SENT_ROWS = 64
AHEAD = 32
LAG = 6
UNITS = 2 * CHUNKS
F32 = jnp.float32
BF16 = jnp.bfloat16


def loop(count, body):
    lax.fori_loop(0, count, lambda i, _: (body(i), None)[1], None)


def kernel(
    slots_ref, feat_ref, tiles_ref, ws_ref, wn_ref, cot_ref,
    hidden_ref, gs_ref, gn_ref,
    src, adj, tbuf_even, tbuf_odd, ws, wn, cot, pre, total, left_self, left_neigh, mean, mean_in,
    rinv, table, inv_ref, dcat, hid, s1_out, s1_in, acc1, s2_out, s2_in, acc2, s3_in,
    local_sem, tile_sem, hid_sem, fc_sem, fc_recv, f_send, f1_recv, f2_recv, f3_recv,
    m_send, m_recv, dp_send, dp_recv, rs_send, s1_recv, s2_recv, s3_recv,
):
    b = lax.axis_index("blk")
    g = lax.axis_index("grp")
    z_lo = b // 2
    core = b % 2
    z_hi = g % 2
    y = (g // 2) % 4
    x = g // 8

    def at(bb, gg):
        return (bb, gg)

    core_peer = at(z_lo * 2 + (1 - core), g)
    z_peer = at(3 - b, g)
    hi_peer = at(3 - b, z_hi * (g - 1) + (1 - z_hi) * (g + 1))
    step = 2 - 4 * z_hi
    out_peer = at(b, (g + step + N_GRP) % N_GRP)
    in_peer = at(b, (g - step + N_GRP) % N_GRP)

    def x_peer(d):
        return at(b, ((x + d) % 4) * 8 + y * 2 + z_hi)

    def y_peer(d):
        return at(b, x * 8 + ((y + d) % 4) * 2 + z_hi)

    def z_ring(d):
        lo = (z_lo + d % 2) % 2
        hi = (z_hi + d // 2) % 2
        return lo, hi

    def z_dev(d):
        lo, hi = z_ring(d)
        return at(lo * 2 + core, x * 8 + y * 2 + hi)

    peers = [core_peer, z_peer, hi_peer, out_peer, in_peer]
    for d in (2, 1, 3):
        peers += [x_peer(d), y_peer(d), z_dev(d)]

    def feat_copy(c):
        return pltpu.make_async_copy(
            feat_ref.at[:, pl.ds(c * COLS, COLS)], src.at[0, c], local_sem.at[c])

    tile_bufs = (tbuf_even, tbuf_odd)

    def tile_copy(r, slot):
        return pltpu.make_async_copy(
            tiles_ref.at[r], tile_bufs[slot].at[pl.ds(0, SLOTS)], tile_sem.at[slot])

    ws_copy = pltpu.make_async_copy(ws_ref, ws, local_sem.at[4])
    wn_copy = pltpu.make_async_copy(wn_ref, wn, local_sem.at[5])
    cot_copy = pltpu.make_async_copy(cot_ref, cot, local_sem.at[6])

    barrier = pltpu.get_barrier_semaphore()
    for p in peers:
        pl.semaphore_signal(barrier, inc=1, device_id=p, device_id_type=MESH)
    tile_copy(0, 0).start()
    tile_copy(1, 1).start()
    for c in range(CHUNKS):
        feat_copy(c).start()
    pl.semaphore_wait(barrier, len(peers))

    def piece(p):
        count = ROWS // SENT_ROWS
        return p // count, pl.ds(pl.multiple_of((p % count) * SENT_ROWS, SENT_ROWS), SENT_ROWS)

    def f1(p):
        c, rows = piece(p)
        return pltpu.make_async_remote_copy(
            src_ref=feat_ref.at[rows, pl.ds(pl.multiple_of(c * COLS, COLS), COLS)],
            dst_ref=src.at[2, c, rows],
            send_sem=f_send.at[0], recv_sem=f1_recv.at[p],
            device_id=z_peer, device_id_type=MESH)

    def f2(p):
        c, rows = piece(p)
        return pltpu.make_async_remote_copy(
            src_ref=src.at[2, c, rows], dst_ref=src.at[3, c, rows],
            send_sem=f_send.at[1], recv_sem=f2_recv.at[p],
            device_id=hi_peer, device_id_type=MESH)

    def f3(p):
        c, rows = piece(p)
        return pltpu.make_async_remote_copy(
            src_ref=src.at[3, c, rows], dst_ref=src.at[4, c, rows],
            send_sem=f_send.at[2], recv_sem=f3_recv.at[p],
            device_id=out_peer, device_id_type=MESH)

    def fc(c):
        return pltpu.make_async_remote_copy(
            src_ref=feat_ref.at[:, pl.ds(pl.multiple_of(c * COLS, COLS), COLS)],
            dst_ref=src.at[1, c],
            send_sem=fc_sem.at[c], recv_sem=fc_recv.at[c],
            device_id=core_peer, device_id_type=MESH)

    for p in range(AHEAD):
        f1(p).start()
    fc(0).start()
    ws_copy.start()
    zero_tile = jnp.zeros((BLOCK, BLOCK), BF16)
    tbuf_even[SLOTS] = zero_tile
    tbuf_odd[SLOTS] = zero_tile

    def find_slots():
        here = b * N_GRP + g
        devices = (here, here + (1 - 2 * core) * N_GRP, (3 - b) * N_GRP + g,
                   here + 1 - 2 * z_hi, b * N_GRP + (g - 1 + 2 * z_hi + N_GRP) % N_GRP)
        named = slots_ref[...]
        owner = named // BLOCKS
        column = jnp.full(named.shape, BLOCK, jnp.int32)
        for s, device in enumerate(devices):
            column = jnp.where(owner == device, s * BLOCKS + named % BLOCKS, column)
        lane = lax.broadcasted_iota(jnp.int32, (BLOCKS, BLOCK), 1)
        found = jnp.full((BLOCKS, BLOCK), SLOTS, jnp.int32)
        for k in reversed(range(SLOTS)):
            found = jnp.where(column[:, k:k + 1] == lane, k, found)
        table[...] = found
        copy = pltpu.make_async_copy(table, inv_ref, local_sem.at[7])
        copy.start()
        copy.wait()

    def build(r, slot):
        tbuf = tile_bufs[slot]

        tile_copy(r, slot).wait()
        rows = pl.ds(pl.multiple_of(r * BLOCK, BLOCK), BLOCK)

        def add(k, acc):
            for n in range(4):
                acc = acc + tbuf[4 * k + n].astype(F32)
            return acc

        deg = lax.fori_loop(0, SLOTS // 4, add, jnp.zeros((BLOCK, BLOCK), F32))
        deg = jnp.sum(deg, axis=1, keepdims=True)
        rinv[rows, :] = jnp.broadcast_to(1.0 / deg, (BLOCK, BLOCK))

        def place(s):
            for j in range(BLOCKS):
                k = inv_ref[r, s * BLOCKS + j]
                adj[s, rows, j * BLOCK:(j + 1) * BLOCK] = tbuf[k]

        loop(5, place)

        @pl.when(r + 2 < BLOCKS)
        def _():
            tile_copy(r + 2, slot).start()

    def product(s, c, first):
        part = jnp.dot(adj[s], src[s, c], preferred_element_type=F32)
        if first:
            total[c] = part
        else:
            total[c] += part

    def chunk(c):
        return pl.ds(pl.multiple_of(c * COLS, COLS), COLS)

    def pre_self(c):
        part = jnp.dot(src[0, c], ws[chunk(c), :], preferred_element_type=F32)
        for q in range(CHUNKS):
            pre[q] += part[:, q * COLS:(q + 1) * COLS]

    def pre_neigh(c):
        part = jnp.dot(mean[c], wn[chunk(c), :], preferred_element_type=F32)
        for q in range(CHUNKS):
            @pl.when(c == 0)
            def _():
                pre[q] = part[:, q * COLS:(q + 1) * COLS]

            @pl.when(c > 0)
            def _():
                pre[q] += part[:, q * COLS:(q + 1) * COLS]

    def half(lo):
        return slice(lo * COLS, (lo + 1) * COLS)

    def flip_self(lo):
        left_self[half(lo), :ROWS] = src[0, 2 * lo + core].T

    def flip_self_partner(lo):
        left_self[half(lo), ROWS:] = src[1, 2 * lo + core].T

    def flip_neigh(lo):
        left_neigh[half(lo), :ROWS] = mean[2 * lo + core].T

    def mean_copy(lo):
        return pltpu.make_async_remote_copy(
            src_ref=mean.at[2 * lo + 1 - core], dst_ref=mean_in.at[lo],
            send_sem=m_send.at[lo], recv_sem=m_recv.at[lo],
            device_id=core_peer, device_id_type=MESH)

    def flip_neigh_partner(lo):
        mean_copy(lo).wait_recv()
        left_neigh[half(lo), ROWS:] = mean_in[lo].T

    def average(c):
        def scale(m):
            rows = pl.ds(pl.multiple_of(m * 256, 256), 256)
            r = rinv[rows, :]
            value = (total[c, rows, :] * jnp.concatenate([r, r], axis=1)).astype(BF16)
            mean[c, rows, :] = value
        loop(4, scale)

        @pl.when(c % 2 != core)
        def _():
            mean_copy(c // 2).start()

    def tick(t):
        @pl.when(t < SENT)
        def _():
            f1(t).wait_recv()
            f2(t).start()

        @pl.when(t + AHEAD < SENT)
        def _():
            f1(t + AHEAD).start()

        @pl.when((t >= LAG) & (t < SENT + LAG))
        def _():
            f2(t - LAG).wait_recv()
            f3(t - LAG).start()

        @pl.when(t >= 2 * LAG)
        def _():
            f3(t - 2 * LAG).wait_recv()

        @pl.when(t % 2 == 1)
        def _():
            jobs(t // 2)

    def jobs(t):
        phase = t // 8
        i = t % 8

        @pl.when((t < 8) & (t % 2 == 0))
        def _():
            build(t, 0)

        @pl.when((t < 8) & (t % 2 == 1))
        def _():
            build(t, 1)

        @pl.when((t == 8) | ((t >= 8) & (t < PIECES) & (i == 1)))
        def _():
            product(0, phase - (t == 8).astype(jnp.int32), True)

        @pl.when((t == 10) | ((t >= 8) & (t < PIECES) & (i == 4)))
        def _():
            c = phase - (t == 10).astype(jnp.int32)
            fc(c).wait_recv()
            product(1, c, False)

        @pl.when((t >= 8) & (t < PIECES + 5) & ((i == 0) | (i == 3) | (i == 5)))
        def _():
            product(2 + i // 2, phase - 1, False)

        @pl.when((t == PIECES + 2) | (t == PIECES + 5))
        def _():
            rows = pl.ds(pl.multiple_of((t - PIECES - 2) // 3 * 512, 512), 512)
            total[CHUNKS - 1] += jnp.dot(
                adj[4, :, rows], src[4, CHUNKS - 1, rows, :], preferred_element_type=F32)

        @pl.when((t >= 4) & (t < PIECES - 8) & (i == 4))
        def _():
            fc(phase + 1).start()

        @pl.when(t == 6)
        def _():
            wn_copy.start()

        @pl.when(t == 12)
        def _():
            ws_copy.wait()

        @pl.when((t == 18) | (t == 26) | (t == 34) | (t == 36))
        def _():
            pre_self(phase - 2 + t // 36)

        @pl.when(t == 14)
        def _():
            flip_self(0)

        @pl.when(t == 22)
        def _():
            flip_self(1)

        @pl.when(t == 30)
        def _():
            flip_self_partner(0)

        @pl.when(t == 20)
        def _():
            cot_copy.start()

        @pl.when(t == 33)
        def _():
            flip_self_partner(1)

        @pl.when(t == 34)
        def _():
            flip_neigh(0)
            flip_neigh_partner(0)

        @pl.when((t >= 8) & (t < PIECES) & (i == 6))
        def _():
            average(phase - 1)

        @pl.when((t >= 8) & (t < PIECES) & (i == 7))
        def _():
            @pl.when(t == 15)
            def _():
                wn_copy.wait()

            pre_neigh(phase - 1)

    for c in range(CHUNKS):
        feat_copy(c).wait()
    find_slots()
    loop(SENT + 2 * LAG, tick)
    average(CHUNKS - 1)
    cot_copy.wait()

    c0 = 0.7978845608028654
    c1 = 0.044715

    def hid_copy(q):
        return pltpu.make_async_copy(
            hid.at[q], hidden_ref.at[:, pl.ds(pl.multiple_of(q * COLS, COLS), COLS)],
            hid_sem.at[q])

    def dp_copy(q):
        return pltpu.make_async_remote_copy(
            src_ref=dcat.at[q, pl.ds(0, ROWS)], dst_ref=dcat.at[q, pl.ds(ROWS, ROWS)],
            send_sem=dp_send.at[q], recv_sem=dp_recv.at[q],
            device_id=core_peer, device_id_type=MESH)

    def gelu(q):
        pre[q] += jnp.dot(
            mean[CHUNKS - 1], wn[DIM - COLS:, q * COLS:(q + 1) * COLS], preferred_element_type=F32)
        for m in range(16):
            rows = slice(m * 64, m * 64 + 64)
            v = pre[q, rows, :]
            p = (c0 * c1) * (v * v)
            th = jnp.tanh(v * (c0 + p))
            upper = 0.5 + 0.5 * th
            out = v * upper
            hid[q, rows, :] = out.astype(BF16)
            slope = upper + out * (1.0 - th) * (c0 + 3.0 * p)
            given = cot[rows, q * COLS:(q + 1) * COLS].astype(F32)
            dcat[q, rows, :] = (given * slope).astype(BF16)
        dp_copy(q).start()
        hid_copy(q).start()

    FIRST = "xyzxyzxy"

    def peer(axis, d):
        return {"x": x_peer, "y": y_peer, "z": z_dev}[axis](d)

    def kept(u, first, count):
        return total[u // 2, pl.ds(pl.multiple_of((u % 2) * 512 + first, 8), count), :]

    def share(u, d):
        axis = FIRST[u]
        if axis == "x":
            pos = (x + d) % 4
            return jnp.concatenate([kept(u, lo * 256 + pos * 64, 64) for lo in range(2)], axis=0)
        if axis == "y":
            pos = (y + d) % 4
            return jnp.concatenate(
                [kept(u, lo * 256 + xx * 64 + pos * 16, 16) for lo in range(2) for xx in range(4)],
                axis=0)
        lo, hi = z_ring(d)
        return jnp.concatenate(
            [kept(u, lo * 256 + k * 16 + hi * 8, 8) for k in range(16)], axis=0)

    def s1(u, d):
        return pltpu.make_async_remote_copy(
            src_ref=s1_out.at[u, d - 1], dst_ref=s1_in.at[u, d - 1],
            send_sem=rs_send.at[0], recv_sem=s1_recv.at[u, d - 1],
            device_id=peer(FIRST[u], d), device_id_type=MESH)

    def second(u):
        return {"x": "z", "y": "z", "z": "x"}[FIRST[u]]

    def third(u):
        return {"x": "y", "y": "x", "z": "y"}[FIRST[u]]

    def place(axis, d):
        if axis == "z":
            lo, hi = z_ring(d)
            return lo * 2 + hi
        return ((x if axis == "x" else y) + d) % 4

    def s2(u, d):
        return pltpu.make_async_remote_copy(
            src_ref=s2_out.at[u, d - 1], dst_ref=s2_in.at[u, d - 1],
            send_sem=rs_send.at[1], recv_sem=s2_recv.at[u, d - 1],
            device_id=peer(second(u), d), device_id_type=MESH)

    def s3(u, d):
        return pltpu.make_async_remote_copy(
            src_ref=acc2.at[u, pl.ds(pl.multiple_of(place(third(u), d) * 8, 8), 8)],
            dst_ref=s3_in.at[u, d - 1],
            send_sem=rs_send.at[2], recv_sem=s3_recv.at[u, d - 1],
            device_id=peer(third(u), d), device_id_type=MESH)

    def gradient(q, kind):
        left = left_self if kind == 0 else left_neigh
        total[q, kind * 512:kind * 512 + 512, :] = jnp.dot(
            left[...], dcat[q], preferred_element_type=F32)

    def stage1(u):
        for d in (2, 1, 3):
            s1_out[u, d - 1] = share(u, d).astype(BF16)
            s1(u, d).start()

    def part2(u, d):
        if FIRST[u] == "z":
            pos = place(second(u), d)
            return acc1[u, pl.ds(pl.multiple_of(pos * 32, 32), 32), :]
        lo, hi = z_ring(d)
        return jnp.concatenate(
            [acc1[u, pl.ds(pl.multiple_of(lo * 64 + k * 16 + hi * 8, 8), 8), :] for k in range(4)],
            axis=0)

    def stage2(u):
        acc = share(u, 0)
        for d in (2, 1, 3):
            s1(u, d).wait_recv()
            acc = acc + s1_in[u, d - 1].astype(F32)
        acc1[u] = acc
        for d in (2, 1, 3):
            s2_out[u, d - 1] = part2(u, d).astype(BF16)
            s2(u, d).start()

    def stage3(u):
        acc = part2(u, 0)
        for d in (2, 1, 3):
            s2(u, d).wait_recv()
            acc = acc + s2_in[u, d - 1].astype(F32)
        acc2[u] = acc
        for d in (2, 1, 3):
            s3(u, d).start()

    def stage4(u):
        out = gs_ref if u % 2 == 0 else gn_ref
        acc = acc2[u, pl.ds(pl.multiple_of(place(third(u), 0) * 8, 8), 8), :]
        for d in (2, 1, 3):
            s3(u, d).wait_recv()
            acc = acc + s3_in[u, d - 1]
        out[:, (u // 2) * COLS:(u // 2 + 1) * COLS] = acc

    gelu(0)
    gelu(1)
    flip_neigh(1)
    for q in range(CHUNKS):
        if 0 < q < CHUNKS - 1:
            gelu(q + 1)
        dp_copy(q).wait_recv()
        gradient(q, 0)
        stage1(2 * q)
        if q == 0:
            flip_neigh_partner(1)
        gradient(q, 1)
        stage1(2 * q + 1)
        if q == 2:
            stage2(0)
            stage2(1)
    for u in (2, 3, 4):
        stage2(u)
    stage3(0)
    stage3(1)
    for u in (5, 6, 7):
        stage2(u)
    for u in range(2, UNITS):
        stage3(u)
    for u in range(UNITS):
        stage4(u)

    for i in range(3):
        pltpu.make_async_copy(src.at[i + 2], src.at[i + 2], f_send.at[i]).wait()
    for i, whole in enumerate((s1_out, s2_out, s3_in)):
        pltpu.make_async_copy(whole, whole, rs_send.at[i]).wait()
    for lo in range(2):
        mean_copy(lo).wait_send()
    for q in range(CHUNKS):
        fc(q).wait_send()
        dp_copy(q).wait_send()
        hid_copy(q).wait()


def fused(slots, features, tiles, w_self, w_neigh, cotangent):
    any_space = pl.BlockSpec(memory_space=pl.ANY)
    vmem = pl.BlockSpec(memory_space=pltpu.VMEM)
    dma = pltpu.SemaphoreType.DMA
    scratch = [
        pltpu.VMEM((5, CHUNKS, ROWS, COLS), BF16),
        pltpu.VMEM((5, ROWS, ROWS), BF16),
        pltpu.VMEM((SLOTS + 1, BLOCK, BLOCK), BF16),
        pltpu.VMEM((SLOTS + 1, BLOCK, BLOCK), BF16),
        pltpu.VMEM((DIM, DIM), BF16),
        pltpu.VMEM((DIM, DIM), BF16),
        pltpu.VMEM((ROWS, DIM), BF16),
        pltpu.VMEM((CHUNKS, ROWS, COLS), F32),
        pltpu.VMEM((CHUNKS, ROWS, COLS), F32),
        pltpu.VMEM((DIM // 2, 2 * ROWS), BF16),
        pltpu.VMEM((DIM // 2, 2 * ROWS), BF16),
        pltpu.VMEM((CHUNKS, ROWS, COLS), BF16),
        pltpu.VMEM((2, ROWS, COLS), BF16),
        pltpu.VMEM((ROWS, BLOCK), F32),
        pltpu.VMEM((BLOCKS, BLOCK), jnp.int32),
        pltpu.SMEM((BLOCKS, BLOCK), jnp.int32),
        pltpu.VMEM((CHUNKS, 2 * ROWS, COLS), BF16),
        pltpu.VMEM((CHUNKS, ROWS, COLS), BF16),
        pltpu.VMEM((UNITS, 3, 128, COLS), BF16),
        pltpu.VMEM((UNITS, 3, 128, COLS), BF16),
        pltpu.VMEM((UNITS, 128, COLS), F32),
        pltpu.VMEM((UNITS, 3, 32, COLS), BF16),
        pltpu.VMEM((UNITS, 3, 32, COLS), BF16),
        pltpu.VMEM((UNITS, 32, COLS), F32),
        pltpu.VMEM((UNITS, 3, 8, COLS), F32),
        dma((8,)), dma((2,)), dma((CHUNKS,)), dma((CHUNKS,)), dma((CHUNKS,)),
        dma((3,)), dma((SENT,)), dma((SENT,)), dma((SENT,)),
        dma((2,)), dma((2,)), dma((CHUNKS,)), dma((CHUNKS,)), dma((3,)),
        dma((UNITS, 3)), dma((UNITS, 3)), dma((UNITS, 3)),
    ]
    return pl.pallas_call(
        kernel,
        out_shape=(
            jax.ShapeDtypeStruct((ROWS, DIM), BF16),
            jax.ShapeDtypeStruct((8, DIM), F32),
            jax.ShapeDtypeStruct((8, DIM), F32),
        ),
        in_specs=[vmem] + [any_space] * 5,
        out_specs=(any_space, vmem, vmem),
        scratch_shapes=scratch,
        compiler_params=pltpu.CompilerParams(
            collective_id=0, has_side_effects=True, vmem_limit_bytes=62 * 1024 * 1024),
        cost_estimate=pl.CostEstimate(
            flops=20_000_000_000, bytes_accessed=20_000_000, transcendentals=1_000_000),
    )(slots, features, tiles, w_self, w_neigh, cotangent)


def settle_kernel(hid_ref, gs_ref, gn_ref, hid_out, gs_out, gn_out, buf, gbuf, sem):
    ways = [(hid_ref.at[pl.ds(i * BLOCK, BLOCK)], buf.at[pl.ds(i * BLOCK, BLOCK)],
             hid_out.at[pl.ds(i * BLOCK, BLOCK)]) for i in range(BLOCKS)]
    ways += [(gs_ref, gbuf.at[0], gs_out), (gn_ref, gbuf.at[1], gn_out)]
    first = [pltpu.make_async_copy(a, m, sem.at[0, i]) for i, (a, m, _) in enumerate(ways)]
    last = [pltpu.make_async_copy(m, c, sem.at[1, i]) for i, (_, m, c) in enumerate(ways)]
    for copy in first:
        copy.start()
    for one, two in zip(first, last):
        one.wait()
        two.start()
    for copy in last:
        copy.wait()


def settled(hidden, grad_self, grad_neigh):
    outs = (hidden, grad_self, grad_neigh)
    return pl.pallas_call(
        settle_kernel,
        out_shape=tuple(jax.ShapeDtypeStruct(a.shape, a.dtype) for a in outs),
        in_specs=[pl.BlockSpec(memory_space=pl.ANY)] * 3,
        out_specs=(pl.BlockSpec(memory_space=pl.ANY),) * 3,
        scratch_shapes=[
            pltpu.VMEM((ROWS, DIM), BF16), pltpu.VMEM((2, 8, DIM), F32),
            pltpu.SemaphoreType.DMA((2, BLOCKS + 2))],
        compiler_params=pltpu.CompilerParams(vmem_limit_bytes=62 * 1024 * 1024),
        cost_estimate=pl.CostEstimate(flops=0, bytes_accessed=4_300_000, transcendentals=0),
    )(*outs)


def on_device(features, tiles, slots, w_self, w_neigh, cotangent):
    return settled(*fused(slots, features, tiles, w_self, w_neigh, cotangent))


def solution(mesh):
    in_specs = (
        P(("blk", "grp"), None),
        P(("blk", "grp"), None, None, None),
        P(("blk", "grp"), None),
        P(),
        P(),
        P(("blk", "grp"), None),
    )
    out_specs = (P(("blk", "grp"), None), P(("blk", "grp"), None), P(("blk", "grp"), None))
    return jax.shard_map(
        on_device, mesh=mesh, in_specs=in_specs, out_specs=out_specs, check_vma=False
    )
```
